32 devices in a mesh: dp: 8 (over z, y), seq: 4 (over x, core).
Axes of the slice: x: 2, y: 2, z: 4, core: 2. Of those that a mesh axis runs over, the one named last changes fastest.
Arguments:
- activations: bfloat16 [16384, 5120], P(('dp', 'seq')), may hold values from -6 to 6
- out_grads: bfloat16 [16384, 5120], P(('dp', 'seq')), may hold values from -6 to 6
- proj_in: bfloat16 [64, 5120], replicated, may hold values from -0.078125 to 0.078125
- proj_out: bfloat16 [128, 5120], replicated, may hold values from -0.078125 to 0.078125
- queries: float32 [128, 8192], P(('dp', 'seq')), may hold values from -3 to 3
- basis_a: float32 [64, 64], replicated, may hold values from -0.75 to 0.75
- basis_g: float32 [128, 128], replicated, may hold values from -0.5 to 0.5
- eigen: float32 [64, 128], replicated, may hold values from 0.05 to 5
- spans: int32 [8, 4, 4], P('dp'), may hold values from 1 to 320, 512 in all within a row
- doc_owner: int32 [8, 4], P('dp'), may hold values from 0 to 7, as said below
- doc_lengths: int32 [8, 4], P('dp'), may hold values from 1280 to 5120
Outputs:
- influence: float32 [8, 8, 128], P('dp', None, 'seq')
The draws below stay inside these ranges and needn't reach their ends.
Inputs may be any that keep to these rules, and one draw needn't show every extreme that they name: In every row spans[j, s, :] the 4 entries sum to 512, and the largest is exactly 320. The 4 owners in each row doc_owner[j, :] differ from one another, and one owner is named in every row.
All inputs are finite; a program needn't handle non-finite values.
Results may differ from the reference program's by a relative error of at most 0.0058.
Values may be sent and summed in bfloat16 or wider, within the bound.
No kernel may reach another device: no remote copies, remote signals or barrier semaphores. Data moves between devices by JAX's collectives and lax.ppermute only.
A program may use at most 64 MiB of HBM per device.

```python
import math
import jax
import jax.numpy as jnp
import numpy as np
from jax import lax

D = 5120
PA = 64
PG = 128
DOC_ROW = 4
TOK_DEV = 512
SPAN_MOST = 320
Q = 128
TOKENS = 16384
N_DP = 8
N_SEQ = 4


def draw_doc_owner(key, part):
    key = jax.random.fold_in(key, 7)
    hot_key, row_key = jax.random.split(key)
    hot_owner = jax.random.randint(hot_key, (1,), 0, N_DP).astype(jnp.int32)

    def one_row(index):
        row = jax.random.fold_in(row_key, index)
        first, second = jax.random.split(row)
        others = jax.random.permutation(first, N_DP - 1)[:DOC_ROW - 1].astype(jnp.int32)
        names = jnp.concatenate([hot_owner, (hot_owner[0] + 1 + others) % N_DP]).astype(jnp.int32)
        order = jax.random.permutation(second, DOC_ROW).astype(jnp.int32)
        return names[order].astype(jnp.int32)
    return jax.vmap(one_row)(jnp.arange(N_DP, dtype=jnp.int32)).astype(jnp.int32)


def set_ends(drawn, key, smallest, high):
    extent = drawn.shape
    spot = [jax.random.randint(jax.random.fold_in(key, axis), (), 0, extent[axis]) for axis in range(len(extent))]
    drawn = drawn.at[tuple(spot)].set(smallest)
    longest = extent.index(max(extent))
    spot[longest] = (spot[longest] + 1) % extent[longest]
    return drawn.at[tuple(spot)].set(high)


def levels(stream_key, shape, cuts, smallest, largest):
    def one(dim, parts):
        heights = jax.random.uniform(jax.random.fold_in(jax.random.fold_in(stream_key, 6), dim), (parts,), jnp.float32, smallest / len(cuts), largest / len(cuts))
        return jnp.repeat(jnp.exp(heights), shape[dim] // parts).reshape((-1,) + (1,) * (len(shape) - dim - 1))

    loudness = one(*cuts[0])
    for cut in cuts[1:]:
        loudness = loudness * one(*cut)
    return loudness


def profile(number_of, total, limit, skew):
    weights = [(1 << 20) // math.isqrt(rank ** skew) + 1 for rank in range(2, number_of + 1)]
    rest, holding = total - limit - (number_of - 1), [1] * (number_of - 1)
    while rest > 0:
        movable = [i for i in range(number_of - 1) if holding[i] < limit]
        pool, remaining = sum([weights[i] for i in movable]), rest
        for i in movable:
            extra = min(limit - holding[i], max(1, remaining * weights[i] // pool), rest)
            holding[i] = holding[i] + extra
            rest = rest - extra
    return np.array([limit] + holding)


def uneven_parts(own_key, count, total, bound, skew):
    if count == 2:
        one = jax.random.randint(own_key, (), max(1, total - bound), min(bound, total - 1) + 1)
        return jnp.stack([one, total - one])
    tallies = jnp.asarray(profile(count, total, bound, skew), jnp.int32)
    twos = (count - 1) // 2
    donor, taker = tallies[1:1 + 2 * twos:2], tallies[2:2 + 2 * twos:2]
    margin = jnp.minimum(donor - 1, bound - taker)
    shifted = jax.random.randint(jax.random.fold_in(own_key, 1), (twos,), 0, 1 << 20) % (margin + 1)
    tallies = tallies.at[1:1 + 2 * twos:2].set(donor - shifted).at[2:2 + 2 * twos:2].set(taker + shifted)
    return tallies[jax.random.permutation(jax.random.fold_in(own_key, 2), count)]


def centred(stream_key, shape, spread, bound, pieces=(), kind=jnp.bfloat16):
    drawn = spread * jax.random.normal(stream_key, shape, jnp.float32)
    if pieces:
        drawn = drawn * levels(stream_key, shape, pieces, -0.22, 0.18)
    return jnp.clip(drawn, -bound, bound).astype(kind)


def setup_inputs(seed: int = 0) -> dict:
    seeds = jax.random.split(jax.random.key(seed), 12)
    activations = centred(seeds[0], (TOKENS, D), 1.0, 6.0, ((0, 32),))
    out_grads = centred(seeds[1], (TOKENS, D), 1.0, 6.0, ((0, 32),))
    proj_in = centred(seeds[2], (PA, D), D ** -0.5, 0.078125)
    proj_out = centred(seeds[3], (PG, D), D ** -0.5, 0.078125)
    queries = centred(seeds[4], (Q, PA * PG), 0.5, 3.0, ((0, 32),), jnp.float32)
    basis_a = centred(seeds[5], (PA, PA), PA ** -0.5, 0.75, (), jnp.float32)
    basis_g = centred(seeds[6], (PG, PG), PG ** -0.5, 0.5, (), jnp.float32)
    eigen = jnp.clip(jnp.exp(jax.random.uniform(seeds[7], (PA, PG), jnp.float32, math.log(0.05), math.log(5.0))), 0.05, 5.0)
    spans = jax.vmap(lambda own: uneven_parts(own, DOC_ROW, TOK_DEV, SPAN_MOST, 2))(jax.random.split(seeds[8], N_DP * N_SEQ)).reshape((N_DP, N_SEQ, DOC_ROW)).astype(jnp.int32)
    doc_owner = draw_doc_owner(jax.random.fold_in(seeds[11], 71), 0)
    doc_lengths = set_ends(jax.random.randint(seeds[10], (N_DP, DOC_ROW), SPAN_MOST * N_SEQ, 4 * SPAN_MOST * N_SEQ + 1), jax.random.fold_in(seeds[10], 1), SPAN_MOST * N_SEQ, 4 * SPAN_MOST * N_SEQ).astype(jnp.int32)
    return {"activations": activations, "out_grads": out_grads, "proj_in": proj_in, "proj_out": proj_out, "queries": queries, "basis_a": basis_a, "basis_g": basis_g, "eigen": eigen, "spans": spans, "doc_owner": doc_owner, "doc_lengths": doc_lengths}


damping = 0.1


def reference(activations, out_grads, proj_in, proj_out, queries, basis_a, basis_g, eigen, spans, doc_owner, doc_lengths):
    grad_width = PA * PG
    act_blocks = activations.reshape(N_DP, N_SEQ, TOK_DEV, -1)
    grad_blocks = out_grads.reshape(N_DP, N_SEQ, TOK_DEV, -1)

    def one_row(packed):
        act_row, grad_row, span_row, length_row = packed

        def add_shard(running, shard_data):
            act_rows, grad_rows, span_shard = shard_data
            a_part = jnp.dot(act_rows, proj_in.T, preferred_element_type=jnp.float32).astype(jnp.bfloat16)
            g_part = jnp.dot(grad_rows, proj_out.T, preferred_element_type=jnp.float32).astype(jnp.bfloat16)
            span_ends = jnp.cumsum(span_shard).astype(jnp.int32)
            position = jnp.arange(TOK_DEV, dtype=jnp.int32)
            doc_index = jnp.sum((position[None, :] >= span_ends[:, None]).astype(jnp.int32), axis=0).astype(jnp.int32)
            outer = (a_part.astype(jnp.float32)[:, :, None] * g_part.astype(jnp.float32)[:, None, :]).reshape(TOK_DEV, grad_width)
            return running + jax.ops.segment_sum(outer, doc_index, num_segments=DOC_ROW), None

        running, _ = lax.scan(add_shard, jnp.zeros((DOC_ROW, grad_width), jnp.float32), (act_row, grad_row, span_row))
        return (running / length_row.astype(jnp.float32)[:, None]).astype(jnp.bfloat16)

    doc_grad = lax.map(one_row, (act_blocks, grad_blocks, spans, doc_lengths))

    highest = lax.Precision.HIGHEST
    query_grid = queries.reshape(-1, PA, PG)
    half_turn = jnp.einsum('ai,nab->nib', basis_a, query_grid, precision=highest)
    rotated = jnp.einsum('nib,bc->nic', half_turn, basis_g, precision=highest)
    scaled = rotated / (eigen + damping)
    returned = jnp.einsum('ai,nic->nac', basis_a, scaled, precision=highest)
    whitened = jnp.einsum('nac,bc->nab', returned, basis_g, precision=highest).reshape(-1, grad_width).astype(jnp.bfloat16)

    score_table = jnp.dot(doc_grad.reshape(-1, grad_width), whitened.T, preferred_element_type=jnp.float32)

    owners = doc_owner.astype(jnp.int32)
    row_ids = jnp.broadcast_to(jnp.arange(N_DP, dtype=jnp.int32)[:, None], owners.shape)
    influence = jnp.zeros((N_DP, N_DP, Q), jnp.float32)
    influence = influence.at[owners.reshape(-1), row_ids.reshape(-1)].set(score_table)
    return influence
```

```python
import functools

import jax
import jax.numpy as jnp
from jax import lax
from jax.experimental import pallas as pl
from jax.experimental.pallas import tpu as pltpu
from jax.sharding import PartitionSpec as P

damping = 0.1
vmem_bytes = 64 * 1024 * 1024
small_bytes = 16 * 1024 * 1024

NT = (((1,), (1,)), ((), ()))
NN = (((1,), (0,)), ((), ()))
TN = (((0,), (0,)), ((), ()))


def whiten_kernel(q_ref, ba_ref, bg_ref, eig_ref, out_ref, rows_ref):
    count = q_ref.shape[0]
    wa, wg = eig_ref.shape
    n_seq = out_ref.shape[1]
    share = wa // n_seq
    dot = functools.partial(
        lax.dot_general,
        precision=lax.Precision.HIGHEST,
        preferred_element_type=jnp.float32,
    )
    for a in range(wa):
        rows_ref[a * count : (a + 1) * count, :] = q_ref[:, a * wg : (a + 1) * wg]
    grid = jnp.concatenate(
        [rows_ref[pl.ds(n, wa, stride=count), :] for n in range(count)], axis=0
    )
    ba, bg = ba_ref[...], bg_ref[...]
    scale = eig_ref[...] + damping
    half = dot(grid, bg, NN)
    back = []
    for n in range(count):
        rotated = dot(ba, half[n * wa : (n + 1) * wa], TN)
        back.append(dot(ba, rotated / scale, NN))
    white = dot(jnp.concatenate(back, axis=0), bg, NT).astype(jnp.bfloat16)
    for n in range(count):
        for s in range(n_seq):
            lo = n * wa + s * share
            block = white[lo : lo + share]
            for o in range(out_ref.shape[0]):
                out_ref[o, s, n] = block


def docs_kernel(
    steps,
    span_hbm,
    owner_hbm,
    length_hbm,
    act_hbm,
    grad_hbm,
    pin_hbm,
    pout_hbm,
    after_hbm,
    out_ref,
    act,
    grad,
    pin,
    pout,
    span_ref,
    owner_ref,
    length_ref,
    sems,
    small_sems,
):
    rows, width = act_hbm.shape
    part = width // steps
    wa = pin_hbm.shape[0]
    n_docs = owner_ref.shape[1]
    n_seq, share, wg = out_ref.shape[1:]
    copies = []
    for k in range(steps):
        cols = pl.ds(k * part, part)
        step = []
        for i, (src, dst) in enumerate(
            ((pin_hbm, pin), (act_hbm, act), (pout_hbm, pout), (grad_hbm, grad))
        ):
            copy = pltpu.make_async_copy(src.at[:, cols], dst.at[k], sems.at[k, i])
            copy.start()
            step.append(copy)
        copies.append(step)
    small = []
    for i, (src, dst) in enumerate(
        ((span_hbm, span_ref), (owner_hbm, owner_ref), (length_hbm, length_ref))
    ):
        copy = pltpu.make_async_copy(src, dst, small_sems.at[i])
        copy.start()
        small.append(copy)
    a_sum = jnp.zeros((rows, wa), jnp.float32)
    g_sum = jnp.zeros((rows, wg), jnp.float32)
    for k in range(steps):
        copies[k][0].wait()
        copies[k][1].wait()
        a_sum += lax.dot_general(
            act[k], pin[k], NT, preferred_element_type=jnp.float32
        )
        copies[k][2].wait()
        copies[k][3].wait()
        g_sum += lax.dot_general(
            grad[k], pout[k], NT, preferred_element_type=jnp.float32
        )
    for copy in small:
        copy.wait()
    a_t = a_sum.T.astype(jnp.bfloat16).astype(jnp.float32)
    g_part = g_sum.astype(jnp.bfloat16)
    me = lax.axis_index("seq")
    position = lax.broadcasted_iota(jnp.int32, (wa, rows), 1)
    start = jnp.int32(0)
    spread = []
    for d in range(n_docs):
        end = start + span_ref[0, me, d]
        inside = (position >= start) & (position < end)
        spread.append(jnp.where(inside, a_t, 0.0).astype(jnp.bfloat16))
        start = end
    sums = jnp.dot(
        jnp.concatenate(spread, axis=0), g_part, preferred_element_type=jnp.float32
    )
    out_ref[...] = jnp.zeros_like(out_ref)
    for d in range(n_docs):
        length = jnp.full((wa, wg), length_ref[0, d], jnp.int32).astype(jnp.float32)
        doc = (sums[d * wa : (d + 1) * wa] / length).astype(jnp.bfloat16)
        out_ref[owner_ref[0, d]] = doc.reshape(n_seq, share, wg)


def score_kernel(docs_ref, white_ref, *refs):
    out_refs, sum_ref = refs[:-1], refs[-1]
    n_dp, n_seq, share, wg = docs_ref.shape
    count = white_ref.shape[0]
    n_out = out_refs[0].shape[1]
    width = n_dp * share
    total = docs_ref[:, 0].astype(jnp.float32)
    for s in range(1, n_seq):
        total += docs_ref[:, s].astype(jnp.float32)
    docs = total.reshape(width, wg).astype(jnp.bfloat16)
    white = white_ref[...].reshape(count * share, wg)
    cross = lax.dot_general(white, docs, NT, preferred_element_type=jnp.float32)
    cross = cross.reshape(count, share, width)
    row = lax.broadcasted_iota(jnp.int32, (share, width), 0)
    col = lax.broadcasted_iota(jnp.int32, (share, width), 1)
    same = (row == col % share)[None]
    sum_ref[...] = jnp.sum(jnp.where(same, cross, 0.0), axis=1)
    owner = lax.broadcasted_iota(jnp.int32, (n_dp, width), 0)
    lane = lax.broadcasted_iota(jnp.int32, (n_dp, width), 1)
    gather = (lane // share == owner).astype(jnp.float32)
    me = lax.axis_index("seq")
    for k in range(n_seq):
        block = sum_ref[pl.ds((me ^ k) * n_out, n_out), :]
        out_refs[k][...] = lax.dot_general(
            gather,
            block,
            NT,
            precision=lax.Precision.HIGHEST,
            preferred_element_type=jnp.float32,
        )


def column_chunks(width):
    weights = (5, 5, 4, 3, 2, 1)
    unit = width // sum(weights)
    if unit * sum(weights) != width or unit % 128:
        return ((0, width),)
    chunks, lo = [], 0
    for weight in weights:
        chunks.append((lo, lo + weight * unit))
        lo += weight * unit
    return tuple(chunks)


def features_kernel(chunks, n_dp, *refs):
    hbm_refs, out_ref, vmem_refs = refs[:11], refs[11], refs[12:23]
    rows_ref, order_ref, placed_ref, small_sems, sems = refs[23:]
    q, ba_ref, bg_ref, eig_ref, span, owner, length, act, grad, pin, pout = vmem_refs
    bf16, f32 = jnp.bfloat16, jnp.float32
    count = q.shape[0]
    wa, wg = eig_ref.shape
    rows = act.shape[0]
    n_docs = owner.shape[1]
    n_dev = n_dp * lax.axis_size("seq")
    height = out_ref.shape[0] // n_dev
    share = wa // n_dev
    high = functools.partial(
        lax.dot_general,
        precision=lax.Precision.HIGHEST,
        preferred_element_type=f32,
    )
    dot = functools.partial(lax.dot_general, preferred_element_type=f32)

    small = []
    for i in range(7):
        copy = pltpu.make_async_copy(hbm_refs[i], vmem_refs[i], small_sems.at[i])
        copy.start()
        small.append(copy)
    copies = []
    for k, (lo, hi) in enumerate(chunks):
        step = []
        for i in (2, 0, 3, 1):
            copy = pltpu.make_async_copy(
                hbm_refs[7 + i].at[:, lo:hi],
                vmem_refs[7 + i].at[:, lo:hi],
                sems.at[k, i],
            )
            copy.start()
            step.append(copy)
        copies.append(step)
    for copy in small:
        copy.wait()

    for a in range(wa):
        rows_ref[a * count : (a + 1) * count, :] = q[:, a * wg : (a + 1) * wg]
    grid = jnp.concatenate(
        [rows_ref[pl.ds(n, wa, stride=count), :] for n in range(count)], axis=0
    )
    ba, bg = ba_ref[...], bg_ref[...]
    scale = eig_ref[...] + damping
    half = high(grid, bg, NN)
    back = []
    for n in range(count):
        rotated = high(ba, half[n * wa : (n + 1) * wa], TN)
        back.append(high(ba, rotated / scale, NN))
    white = high(jnp.concatenate(back, axis=0), bg, NT).astype(bf16)

    def iota(width, dim):
        return lax.broadcasted_iota(jnp.int32, (height, width), dim)

    first = share * n_dp
    t, col = iota(count * wa, 0), iota(count * wa, 1)
    r, n = lax.div(t - first, count), lax.rem(t - first, count)
    fits = (t >= first) & (lax.div(col, wa) == n)
    base = jnp.where(fits, lax.rem(col, wa) - r, -1)
    picks = [(base == share * f).astype(f32) for f in range(n_dev)]
    order = jnp.concatenate(picks, axis=0).astype(bf16)
    placed_ref[...] = dot(order, white, NN)
    t, col = iota(n_docs * wa, 0), iota(n_docs * wa, 1)
    r, o = lax.div(t, n_dp), lax.rem(t, n_dp)
    doc = lax.div(col, wa)
    doc_owner = jnp.full_like(col, owner[0, 0])
    for d in range(1, n_docs):
        doc_owner = jnp.where(doc == d, owner[0, d], doc_owner)
    fits = (t < first) & (doc_owner == o)
    base = jnp.where(fits, lax.rem(col, wa) - r, -1)
    picks = [(base == share * f).astype(f32) for f in range(n_dev)]
    order_ref[...] = jnp.concatenate(picks, axis=0).astype(bf16)

    a_sum = jnp.zeros((wa, rows), f32)
    g_sum = jnp.zeros((wg, rows), f32)
    for k, (lo, hi) in enumerate(chunks):
        copies[k][0].wait()
        copies[k][1].wait()
        a_sum += dot(pin[:, lo:hi], act[:, lo:hi], NT)
        copies[k][2].wait()
        copies[k][3].wait()
        g_sum += dot(pout[:, lo:hi], grad[:, lo:hi], NT)
    a_part = a_sum.astype(bf16).astype(f32)
    g_part = g_sum.astype(bf16)
    me = lax.axis_index("seq")
    position = lax.broadcasted_iota(jnp.int32, (wa, rows), 1)
    start = jnp.int32(0)
    spread = []
    for d in range(n_docs):
        end = start + span[0, me, d]
        inside = (position >= start) & (position < end)
        spread.append(jnp.where(inside, a_part, 0.0).astype(bf16))
        start = end
    sums = dot(jnp.concatenate(spread, axis=0), g_part, NT)
    docs = []
    for d in range(n_docs):
        tokens = jnp.full((wa, wg), length[0, d], jnp.int32).astype(f32)
        docs.append((sums[d * wa : (d + 1) * wa] / tokens).astype(bf16))
    routed = dot(order_ref[...], jnp.concatenate(docs, axis=0), NN)
    out_ref[...] = (placed_ref[...] + routed).astype(bf16)


def partial_kernel(n_dp, count, block_ref, out_ref):
    bf16, f32 = jnp.bfloat16, jnp.float32
    n_seq = out_ref.shape[1]
    n_hi = out_ref.shape[2]
    n_dev = n_dp * n_seq
    rows, wg = block_ref.shape
    height = rows // n_dev
    share = height // (n_dp + count)
    n_out = n_dev * count // n_seq
    n_lo = n_dp // n_hi
    blocks = block_ref[...].astype(f32).reshape(n_dp, n_seq, height, wg)
    docs, white = [], []
    for r in range(share):
        lo = r * n_dp
        total = blocks[:, 0, lo : lo + n_dp]
        for s in range(1, n_seq):
            total += blocks[:, s, lo : lo + n_dp]
        docs.append(total.reshape(n_dp * n_dp, wg))
        lo = share * n_dp + r * count
        white.append(blocks[:, :, lo : lo + count].reshape(n_dev * count, wg))
    docs = jnp.concatenate(docs, axis=1)
    white = jnp.concatenate(white, axis=1).astype(bf16)
    upper = docs.astype(bf16)
    lower = (docs - upper.astype(f32)).astype(bf16)
    both = lax.dot_general(
        jnp.concatenate([upper, lower], axis=0), white, NT, preferred_element_type=f32
    )
    scores = both[: n_dp * n_dp] + both[n_dp * n_dp :]
    tall = n_hi * n_dp
    for s in range(n_seq):
        lanes = slice(s * n_out, (s + 1) * n_out)
        packed = jnp.concatenate(
            [scores[lo * tall : (lo + 1) * tall, lanes] for lo in range(n_lo)], axis=1
        )
        for hi in range(n_hi):
            out_ref[:, s, hi, :] = packed[hi * n_dp : (hi + 1) * n_dp]


def finish_kernel(parts_ref, out_ref):
    n_hi = parts_ref.shape[1]
    n_dp, n_out = out_ref.shape
    total = jnp.sum(parts_ref[...], axis=0)
    for lo in range(n_dp // n_hi):
        out_ref[lo * n_hi : (lo + 1) * n_hi, :] = total[:, lo * n_out : (lo + 1) * n_out]


def by_features(
    activations,
    out_grads,
    proj_in,
    proj_out,
    queries,
    basis_a,
    basis_g,
    eigen,
    spans,
    doc_owner,
    doc_lengths,
):
    n_dp, n_seq = lax.axis_size("dp"), lax.axis_size("seq")
    n_dev = n_dp * n_seq
    wa, wg = eigen.shape
    count = queries.shape[0]
    share = wa // n_dev
    height = share * (n_dp + count)
    n_out = n_dev * count // n_seq
    n_hi = n_dp * n_out // 128
    bf16, f32 = jnp.bfloat16, jnp.float32
    chunks = column_chunks(activations.shape[1])
    params = pltpu.CompilerParams(vmem_limit_bytes=vmem_bytes)
    vmem = pl.BlockSpec(memory_space=pltpu.VMEM)
    hbm = pl.BlockSpec(memory_space=pltpu.HBM)
    small = (queries, basis_a, basis_g, eigen)
    integers = (spans, doc_owner, doc_lengths)
    large = (activations, out_grads, proj_in, proj_out)
    copied = (
        [pltpu.VMEM(x.shape, x.dtype) for x in small]
        + [pltpu.SMEM(x.shape, x.dtype) for x in integers]
        + [pltpu.VMEM(x.shape, x.dtype) for x in large]
    )
    blocks = pl.pallas_call(
        functools.partial(features_kernel, chunks, n_dp),
        out_shape=jax.ShapeDtypeStruct((n_dev * height, wg), bf16),
        in_specs=[hbm] * 11,
        out_specs=vmem,
        scratch_shapes=copied
        + [
            pltpu.VMEM((wa * count, wg), f32),
            pltpu.VMEM((n_dev * height, doc_owner.shape[1] * wa), bf16),
            pltpu.VMEM((n_dev * height, wg), f32),
            pltpu.SemaphoreType.DMA((7,)),
            pltpu.SemaphoreType.DMA((len(chunks), 4)),
        ],
        compiler_params=params,
        name="features",
    )(*small, *integers, *large)
    everywhere = functools.partial(
        lax.all_to_all,
        axis_name=("dp", "seq"),
        split_axis=0,
        concat_axis=0,
        tiled=True,
    )
    blocks = everywhere(blocks)
    parts = pl.pallas_call(
        functools.partial(partial_kernel, n_dp, count),
        out_shape=jax.ShapeDtypeStruct((n_dp, n_seq, n_hi, 128), f32),
        in_specs=[vmem],
        out_specs=vmem,
        compiler_params=pltpu.CompilerParams(vmem_limit_bytes=small_bytes),
        name="partial",
    )(blocks)
    parts = everywhere(parts.reshape(n_dev, n_hi, 128))
    result = pl.pallas_call(
        finish_kernel,
        out_shape=jax.ShapeDtypeStruct((n_dp, n_out), f32),
        in_specs=[vmem],
        out_specs=vmem,
        compiler_params=pltpu.CompilerParams(vmem_limit_bytes=small_bytes),
        name="finish",
    )(parts)
    return result[None]


def by_rows(
    activations,
    out_grads,
    proj_in,
    proj_out,
    queries,
    basis_a,
    basis_g,
    eigen,
    spans,
    doc_owner,
    doc_lengths,
):
    n_dp, n_seq = lax.axis_size("dp"), lax.axis_size("seq")
    n_dev = n_dp * n_seq
    rows, width = activations.shape
    wa, wg = eigen.shape
    count = queries.shape[0]
    share = wa // n_seq
    steps = 5
    part = width // steps
    bf16, f32 = jnp.bfloat16, jnp.float32
    params = pltpu.CompilerParams(vmem_limit_bytes=vmem_bytes)
    vmem = pl.BlockSpec(memory_space=pltpu.VMEM)
    hbm = pl.BlockSpec(memory_space=pltpu.HBM)

    outgoing = pl.pallas_call(
        whiten_kernel,
        out_shape=jax.ShapeDtypeStruct((n_dp, n_seq, count, share, wg), bf16),
        in_specs=[vmem] * 4,
        out_specs=vmem,
        scratch_shapes=[pltpu.VMEM((wa * count, wg), f32)],
        compiler_params=params,
        name="whiten",
    )(queries, basis_a, basis_g, eigen)
    white = lax.all_to_all(
        outgoing.reshape(n_dev, count, share, wg),
        ("dp", "seq"),
        split_axis=0,
        concat_axis=0,
        tiled=True,
    )

    docs = pl.pallas_call(
        functools.partial(docs_kernel, steps),
        out_shape=jax.ShapeDtypeStruct((n_dp, n_seq, share, wg), bf16),
        in_specs=[hbm] * 8,
        out_specs=vmem,
        scratch_shapes=[
            pltpu.VMEM((steps, rows, part), bf16),
            pltpu.VMEM((steps, rows, part), bf16),
            pltpu.VMEM((steps, wa, part), bf16),
            pltpu.VMEM((steps, wg, part), bf16),
            pltpu.SMEM(spans.shape, jnp.int32),
            pltpu.SMEM(doc_owner.shape, jnp.int32),
            pltpu.SMEM(doc_lengths.shape, jnp.int32),
            pltpu.SemaphoreType.DMA((steps, 4)),
            pltpu.SemaphoreType.DMA((3,)),
        ],
        compiler_params=params,
        name="docs",
    )(
        spans,
        doc_owner,
        doc_lengths,
        activations,
        out_grads,
        proj_in,
        proj_out,
        outgoing,
    )
    docs = lax.all_to_all(
        docs.reshape(n_dev, share, wg),
        ("dp", "seq"),
        split_axis=0,
        concat_axis=0,
        tiled=True,
    )

    n_query = n_dev * count
    n_out = n_query // n_seq
    parts = pl.pallas_call(
        score_kernel,
        out_shape=[jax.ShapeDtypeStruct((n_dp, n_out), f32)] * n_seq,
        in_specs=[vmem] * 2,
        out_specs=[vmem] * n_seq,
        scratch_shapes=[pltpu.VMEM((n_query, n_dp * share), f32)],
        compiler_params=params,
        name="score",
    )(docs.reshape(n_dp, n_seq, share, wg), white.reshape(n_query, share, wg))
    result = parts[0]
    for k in range(n_seq - 1, 0, -1):
        pairs = [(i, i ^ k) for i in range(n_seq)]
        result = result + lax.ppermute(parts[k], "seq", pairs)
    return result[None]


def per_device(*args):
    n_dp, n_seq = lax.axis_size("dp"), lax.axis_size("seq")
    n_dev = n_dp * n_seq
    wa, wg = args[7].shape
    count = args[4].shape[0]
    share = wa // n_dev
    n_out = n_dp * count
    fits = (
        share * n_dev == wa
        and wg == 128
        and n_dp % 8 == 0
        and share * count % 8 == 0
        and 128 % n_out == 0
        and n_dp * n_out % 128 == 0
    )
    return (by_features if fits else by_rows)(*args)


def solution(mesh):
    return jax.shard_map(
        per_device,
        mesh=mesh,
        in_specs=(
            P(("dp", "seq"), None),
            P(("dp", "seq"), None),
            P(),
            P(),
            P(("dp", "seq"), None),
            P(),
            P(),
            P(),
            P("dp", None, None),
            P("dp", None),
            P("dp", None),
        ),
        out_specs=P("dp", None, "seq"),
        check_vma=False,
    )
```

```python
import functools

import jax
import jax.numpy as jnp
from jax import lax
from jax.experimental import pallas as pl
from jax.experimental.pallas import tpu as pltpu
from jax.sharding import PartitionSpec as P

damping = 0.1
vmem_bytes = 64 * 1024 * 1024
small_bytes = 16 * 1024 * 1024

NT = (((1,), (1,)), ((), ()))
NN = (((1,), (0,)), ((), ()))
TN = (((0,), (0,)), ((), ()))


def whiten_kernel(q_ref, ba_ref, bg_ref, eig_ref, out_ref, rows_ref):
    count = q_ref.shape[0]
    wa, wg = eig_ref.shape
    n_seq = out_ref.shape[1]
    share = wa // n_seq
    dot = functools.partial(
        lax.dot_general,
        precision=lax.Precision.HIGHEST,
        preferred_element_type=jnp.float32,
    )
    for a in range(wa):
        rows_ref[a * count : (a + 1) * count, :] = q_ref[:, a * wg : (a + 1) * wg]
    grid = jnp.concatenate(
        [rows_ref[pl.ds(n, wa, stride=count), :] for n in range(count)], axis=0
    )
    ba, bg = ba_ref[...], bg_ref[...]
    scale = eig_ref[...] + damping
    half = dot(grid, bg, NN)
    back = []
    for n in range(count):
        rotated = dot(ba, half[n * wa : (n + 1) * wa], TN)
        back.append(dot(ba, rotated / scale, NN))
    white = dot(jnp.concatenate(back, axis=0), bg, NT).astype(jnp.bfloat16)
    for n in range(count):
        for s in range(n_seq):
            lo = n * wa + s * share
            block = white[lo : lo + share]
            for o in range(out_ref.shape[0]):
                out_ref[o, s, n] = block


def docs_kernel(
    steps,
    span_hbm,
    owner_hbm,
    length_hbm,
    act_hbm,
    grad_hbm,
    pin_hbm,
    pout_hbm,
    after_hbm,
    out_ref,
    act,
    grad,
    pin,
    pout,
    span_ref,
    owner_ref,
    length_ref,
    sems,
    small_sems,
):
    rows, width = act_hbm.shape
    part = width // steps
    wa = pin_hbm.shape[0]
    n_docs = owner_ref.shape[1]
    n_seq, share, wg = out_ref.shape[1:]
    copies = []
    for k in range(steps):
        cols = pl.ds(k * part, part)
        step = []
        for i, (src, dst) in enumerate(
            ((pin_hbm, pin), (act_hbm, act), (pout_hbm, pout), (grad_hbm, grad))
        ):
            copy = pltpu.make_async_copy(src.at[:, cols], dst.at[k], sems.at[k, i])
            copy.start()
            step.append(copy)
        copies.append(step)
    small = []
    for i, (src, dst) in enumerate(
        ((span_hbm, span_ref), (owner_hbm, owner_ref), (length_hbm, length_ref))
    ):
        copy = pltpu.make_async_copy(src, dst, small_sems.at[i])
        copy.start()
        small.append(copy)
    a_sum = jnp.zeros((rows, wa), jnp.float32)
    g_sum = jnp.zeros((rows, wg), jnp.float32)
    for k in range(steps):
        copies[k][0].wait()
        copies[k][1].wait()
        a_sum += lax.dot_general(
            act[k], pin[k], NT, preferred_element_type=jnp.float32
        )
        copies[k][2].wait()
        copies[k][3].wait()
        g_sum += lax.dot_general(
            grad[k], pout[k], NT, preferred_element_type=jnp.float32
        )
    for copy in small:
        copy.wait()
    a_t = a_sum.T.astype(jnp.bfloat16).astype(jnp.float32)
    g_part = g_sum.astype(jnp.bfloat16)
    me = lax.axis_index("seq")
    position = lax.broadcasted_iota(jnp.int32, (wa, rows), 1)
    start = jnp.int32(0)
    spread = []
    for d in range(n_docs):
        end = start + span_ref[0, me, d]
        inside = (position >= start) & (position < end)
        spread.append(jnp.where(inside, a_t, 0.0).astype(jnp.bfloat16))
        start = end
    sums = jnp.dot(
        jnp.concatenate(spread, axis=0), g_part, preferred_element_type=jnp.float32
    )
    out_ref[...] = jnp.zeros_like(out_ref)
    for d in range(n_docs):
        length = jnp.full((wa, wg), length_ref[0, d], jnp.int32).astype(jnp.float32)
        doc = (sums[d * wa : (d + 1) * wa] / length).astype(jnp.bfloat16)
        out_ref[owner_ref[0, d]] = doc.reshape(n_seq, share, wg)


def score_kernel(docs_ref, white_ref, *refs):
    out_refs, sum_ref = refs[:-1], refs[-1]
    n_dp, n_seq, share, wg = docs_ref.shape
    count = white_ref.shape[0]
    n_out = out_refs[0].shape[1]
    width = n_dp * share
    total = docs_ref[:, 0].astype(jnp.float32)
    for s in range(1, n_seq):
        total += docs_ref[:, s].astype(jnp.float32)
    docs = total.reshape(width, wg).astype(jnp.bfloat16)
    white = white_ref[...].reshape(count * share, wg)
    cross = lax.dot_general(white, docs, NT, preferred_element_type=jnp.float32)
    cross = cross.reshape(count, share, width)
    row = lax.broadcasted_iota(jnp.int32, (share, width), 0)
    col = lax.broadcasted_iota(jnp.int32, (share, width), 1)
    same = (row == col % share)[None]
    sum_ref[...] = jnp.sum(jnp.where(same, cross, 0.0), axis=1)
    owner = lax.broadcasted_iota(jnp.int32, (n_dp, width), 0)
    lane = lax.broadcasted_iota(jnp.int32, (n_dp, width), 1)
    gather = (lane // share == owner).astype(jnp.float32)
    me = lax.axis_index("seq")
    for k in range(n_seq):
        block = sum_ref[pl.ds((me ^ k) * n_out, n_out), :]
        out_refs[k][...] = lax.dot_general(
            gather,
            block,
            NT,
            precision=lax.Precision.HIGHEST,
            preferred_element_type=jnp.float32,
        )


def split_dot(x, w):
    bf16 = jnp.bfloat16
    x_hi, w_hi = x.astype(bf16), w.astype(bf16)
    x_lo = (x - x_hi.astype(jnp.float32)).astype(bf16)
    w_lo = (w - w_hi.astype(jnp.float32)).astype(bf16)
    return jnp.dot(
        jnp.concatenate([x_hi, x_lo, x_hi], axis=1),
        jnp.concatenate([w_hi, w_hi, w_lo], axis=0),
        preferred_element_type=jnp.float32,
    )


def side_by_side(x, count):
    rows = x.shape[0] // count
    return jnp.concatenate(
        [x[n * rows : (n + 1) * rows] for n in range(count)], axis=1
    )


def features_kernel(steps, n_dp, *refs):
    hbm_refs, out_ref, local_refs = refs[:11], refs[11], refs[12:23]
    rows_ref, a_sum, g_sum, blocks, small_sems, sems = refs[23:]
    q, ba_ref, bg_ref, eig_ref, span, owner, length, act, grad, pin, pout = local_refs
    bf16, f32 = jnp.bfloat16, jnp.float32
    count = q.shape[0]
    wa, wg = eig_ref.shape
    rows, part = act.shape[1:]
    n_docs = owner.shape[1]
    n_dev = out_ref.shape[0]
    share = wa // n_dev
    dot = functools.partial(lax.dot_general, preferred_element_type=f32)

    def chunk(k):
        cols = pl.ds(pl.multiple_of(k * part, part), part)
        return [
            pltpu.make_async_copy(
                hbm_refs[7 + i].at[:, cols], local_refs[7 + i].at[k], sems.at[k, i]
            )
            for i in (2, 0, 3, 1)
        ]

    small = []
    for i in range(7):
        copy = pltpu.make_async_copy(hbm_refs[i], local_refs[i], small_sems.at[i])
        copy.start()
        small.append(copy)
    for copy in chunk(0):
        copy.start()
    a_sum[...] = jnp.zeros_like(a_sum)
    g_sum[...] = jnp.zeros_like(g_sum)
    blocks[: share * n_dp] = jnp.zeros_like(blocks[: share * n_dp])
    def whiten():
        for copy in small[:4]:
            copy.wait()
        for k in range(1, steps):
            for copy in chunk(k):
                copy.start()
        for a in range(wa):
            rows_ref[a * count : (a + 1) * count, :] = q[:, a * wg : (a + 1) * wg]
        grid = jnp.concatenate(
            [rows_ref[pl.ds(n, wa, stride=count), :] for n in range(count)], axis=0
        )
        ba, bg = ba_ref[...], bg_ref[...]
        scale = jnp.concatenate([eig_ref[...] + damping] * count, axis=1)
        rotated = split_dot(ba.T, side_by_side(split_dot(grid, bg), count))
        back = split_dot(ba, rotated / scale)
        back = jnp.concatenate(
            [back[:, n * wg : (n + 1) * wg] for n in range(count)], axis=0
        )
        white = split_dot(back, bg.T)
        for r in range(share):
            for n in range(count):
                lo = n * wa + r * n_dev
                blocks[share * n_dp + r * count + n] = white[lo : lo + n_dev]

    def add_chunk(k, carry):
        for copy in chunk(k):
            copy.wait()
        a_sum[...] += dot(act[k], pin[k], NT)
        g_sum[...] += dot(grad[k], pout[k], NT)
        return carry

    whiten()
    lax.fori_loop(0, steps, add_chunk, 0)
    for copy in small[4:]:
        copy.wait()
    a_part = a_sum[...].T.astype(bf16).astype(f32)
    g_part = g_sum[...].astype(bf16)
    me = lax.axis_index("seq")
    position = lax.broadcasted_iota(jnp.int32, (wa, rows), 1)
    start = jnp.int32(0)
    spread = []
    for d in range(n_docs):
        end = start + span[0, me, d]
        inside = (position >= start) & (position < end)
        spread.append(jnp.where(inside, a_part, 0.0).astype(bf16))
        start = end
    sums = dot(jnp.concatenate(spread, axis=0), g_part, NN)
    for d in range(n_docs):
        tokens = jnp.full((n_dev, wg), length[0, d], jnp.int32).astype(f32)
        for r in range(share):
            lo = d * wa + r * n_dev
            blocks[r * n_dp + owner[0, d]] = sums[lo : lo + n_dev] / tokens
    out_ref[...] = jnp.swapaxes(blocks[...], 0, 1).astype(bf16)


def partial_kernel(n_dp, count, block_ref, out_ref):
    bf16, f32 = jnp.bfloat16, jnp.float32
    n_seq = out_ref.shape[1]
    n_hi = out_ref.shape[2]
    n_dev = n_dp * n_seq
    height, wg = block_ref.shape[1:]
    share = height // (n_dp + count)
    n_out = n_dev * count // n_seq
    n_lo = n_dp // n_hi
    blocks = block_ref[...].astype(f32).reshape(n_dp, n_seq, height, wg)
    docs, white = [], []
    for r in range(share):
        lo = r * n_dp
        total = blocks[:, 0, lo : lo + n_dp]
        for s in range(1, n_seq):
            total += blocks[:, s, lo : lo + n_dp]
        docs.append(total.reshape(n_dp * n_dp, wg))
        lo = share * n_dp + r * count
        white.append(blocks[:, :, lo : lo + count].reshape(n_dev * count, wg))
    docs = jnp.concatenate(docs, axis=1)
    white = jnp.concatenate(white, axis=1).astype(bf16)
    upper = docs.astype(bf16)
    lower = (docs - upper.astype(f32)).astype(bf16)
    both = lax.dot_general(
        jnp.concatenate([upper, lower], axis=0), white, NT, preferred_element_type=f32
    )
    scores = both[: n_dp * n_dp] + both[n_dp * n_dp :]
    tall = n_hi * n_dp
    for s in range(n_seq):
        lanes = slice(s * n_out, (s + 1) * n_out)
        packed = jnp.concatenate(
            [scores[lo * tall : (lo + 1) * tall, lanes] for lo in range(n_lo)], axis=1
        )
        for hi in range(n_hi):
            out_ref[:, s, hi, :] = packed[hi * n_dp : (hi + 1) * n_dp]


def finish_kernel(parts_ref, out_ref):
    n_hi = parts_ref.shape[1]
    n_dp, n_out = out_ref.shape
    total = jnp.sum(parts_ref[...], axis=0)
    for lo in range(n_dp // n_hi):
        out_ref[lo * n_hi : (lo + 1) * n_hi, :] = total[:, lo * n_out : (lo + 1) * n_out]


def by_features(
    activations,
    out_grads,
    proj_in,
    proj_out,
    queries,
    basis_a,
    basis_g,
    eigen,
    spans,
    doc_owner,
    doc_lengths,
):
    n_dp, n_seq = lax.axis_size("dp"), lax.axis_size("seq")
    n_dev = n_dp * n_seq
    wa, wg = eigen.shape
    count = queries.shape[0]
    share = wa // n_dev
    height = share * (n_dp + count)
    n_out = n_dev * count // n_seq
    n_hi = n_dp * n_out // 128
    bf16, f32 = jnp.bfloat16, jnp.float32
    steps = 5
    part = activations.shape[1] // steps
    params = pltpu.CompilerParams(vmem_limit_bytes=vmem_bytes)
    vmem = pl.BlockSpec(memory_space=pltpu.VMEM)
    hbm = pl.BlockSpec(memory_space=pltpu.HBM)
    small = (queries, basis_a, basis_g, eigen)
    integers = (spans, doc_owner, doc_lengths)
    large = (activations, out_grads, proj_in, proj_out)
    copied = (
        [pltpu.VMEM(x.shape, x.dtype) for x in small]
        + [pltpu.SMEM(x.shape, x.dtype) for x in integers]
        + [pltpu.VMEM((steps, x.shape[0], part), x.dtype) for x in large]
    )
    blocks = pl.pallas_call(
        functools.partial(features_kernel, steps, n_dp),
        out_shape=jax.ShapeDtypeStruct((n_dev, height, wg), bf16),
        in_specs=[hbm] * 11,
        out_specs=vmem,
        scratch_shapes=copied
        + [
            pltpu.VMEM((wa * count, wg), f32),
            pltpu.VMEM((activations.shape[0], wa), f32),
            pltpu.VMEM((activations.shape[0], wg), f32),
            pltpu.VMEM((height, n_dev, wg), f32),
            pltpu.SemaphoreType.DMA((7,)),
            pltpu.SemaphoreType.DMA((steps, 4)),
        ],
        compiler_params=params,
        name="features",
    )(*small, *integers, *large)
    everywhere = functools.partial(
        lax.all_to_all,
        axis_name=("dp", "seq"),
        split_axis=0,
        concat_axis=0,
        tiled=True,
    )
    blocks = everywhere(blocks)
    parts = pl.pallas_call(
        functools.partial(partial_kernel, n_dp, count),
        out_shape=jax.ShapeDtypeStruct((n_dp, n_seq, n_hi, 128), f32),
        in_specs=[vmem],
        out_specs=vmem,
        compiler_params=pltpu.CompilerParams(vmem_limit_bytes=small_bytes),
        name="partial",
    )(blocks)
    parts = everywhere(parts.reshape(n_dev, n_hi, 128))
    result = pl.pallas_call(
        finish_kernel,
        out_shape=jax.ShapeDtypeStruct((n_dp, n_out), f32),
        in_specs=[vmem],
        out_specs=vmem,
        compiler_params=pltpu.CompilerParams(vmem_limit_bytes=small_bytes),
        name="finish",
    )(parts)
    return result[None]


def by_rows(
    activations,
    out_grads,
    proj_in,
    proj_out,
    queries,
    basis_a,
    basis_g,
    eigen,
    spans,
    doc_owner,
    doc_lengths,
):
    n_dp, n_seq = lax.axis_size("dp"), lax.axis_size("seq")
    n_dev = n_dp * n_seq
    rows, width = activations.shape
    wa, wg = eigen.shape
    count = queries.shape[0]
    share = wa // n_seq
    steps = 5
    part = width // steps
    bf16, f32 = jnp.bfloat16, jnp.float32
    params = pltpu.CompilerParams(vmem_limit_bytes=vmem_bytes)
    vmem = pl.BlockSpec(memory_space=pltpu.VMEM)
    hbm = pl.BlockSpec(memory_space=pltpu.HBM)

    outgoing = pl.pallas_call(
        whiten_kernel,
        out_shape=jax.ShapeDtypeStruct((n_dp, n_seq, count, share, wg), bf16),
        in_specs=[vmem] * 4,
        out_specs=vmem,
        scratch_shapes=[pltpu.VMEM((wa * count, wg), f32)],
        compiler_params=params,
        name="whiten",
    )(queries, basis_a, basis_g, eigen)
    white = lax.all_to_all(
        outgoing.reshape(n_dev, count, share, wg),
        ("dp", "seq"),
        split_axis=0,
        concat_axis=0,
        tiled=True,
    )

    docs = pl.pallas_call(
        functools.partial(docs_kernel, steps),
        out_shape=jax.ShapeDtypeStruct((n_dp, n_seq, share, wg), bf16),
        in_specs=[hbm] * 8,
        out_specs=vmem,
        scratch_shapes=[
            pltpu.VMEM((steps, rows, part), bf16),
            pltpu.VMEM((steps, rows, part), bf16),
            pltpu.VMEM((steps, wa, part), bf16),
            pltpu.VMEM((steps, wg, part), bf16),
            pltpu.SMEM(spans.shape, jnp.int32),
            pltpu.SMEM(doc_owner.shape, jnp.int32),
            pltpu.SMEM(doc_lengths.shape, jnp.int32),
            pltpu.SemaphoreType.DMA((steps, 4)),
            pltpu.SemaphoreType.DMA((3,)),
        ],
        compiler_params=params,
        name="docs",
    )(
        spans,
        doc_owner,
        doc_lengths,
        activations,
        out_grads,
        proj_in,
        proj_out,
        outgoing,
    )
    docs = lax.all_to_all(
        docs.reshape(n_dev, share, wg),
        ("dp", "seq"),
        split_axis=0,
        concat_axis=0,
        tiled=True,
    )

    n_query = n_dev * count
    n_out = n_query // n_seq
    parts = pl.pallas_call(
        score_kernel,
        out_shape=[jax.ShapeDtypeStruct((n_dp, n_out), f32)] * n_seq,
        in_specs=[vmem] * 2,
        out_specs=[vmem] * n_seq,
        scratch_shapes=[pltpu.VMEM((n_query, n_dp * share), f32)],
        compiler_params=params,
        name="score",
    )(docs.reshape(n_dp, n_seq, share, wg), white.reshape(n_query, share, wg))
    result = parts[0]
    for k in range(n_seq - 1, 0, -1):
        pairs = [(i, i ^ k) for i in range(n_seq)]
        result = result + lax.ppermute(parts[k], "seq", pairs)
    return result[None]


def per_device(*args):
    n_dp, n_seq = lax.axis_size("dp"), lax.axis_size("seq")
    n_dev = n_dp * n_seq
    wa, wg = args[7].shape
    count = args[4].shape[0]
    share = wa // n_dev
    n_out = n_dp * count
    fits = (
        share * n_dev == wa
        and wg == 128
        and n_dp % 8 == 0
        and share * count % 8 == 0
        and 128 % n_out == 0
        and n_dp * n_out % 128 == 0
    )
    return (by_features if fits else by_rows)(*args)


def solution(mesh):
    return jax.shard_map(
        per_device,
        mesh=mesh,
        in_specs=(
            P(("dp", "seq"), None),
            P(("dp", "seq"), None),
            P(),
            P(),
            P(("dp", "seq"), None),
            P(),
            P(),
            P(),
            P("dp", None, None),
            P("dp", None),
            P("dp", None),
        ),
        out_specs=P("dp", None, "seq"),
        check_vma=False,
    )
```

```python
import functools

import jax
import jax.numpy as jnp
from jax import lax
from jax.experimental import pallas as pl
from jax.experimental.pallas import tpu as pltpu
from jax.sharding import PartitionSpec as P

damping = 0.1
vmem_bytes = 64 * 1024 * 1024
small_bytes = 16 * 1024 * 1024

NT = (((1,), (1,)), ((), ()))
NN = (((1,), (0,)), ((), ()))
TN = (((0,), (0,)), ((), ()))


def whiten_kernel(q_ref, ba_ref, bg_ref, eig_ref, out_ref, rows_ref):
    count = q_ref.shape[0]
    wa, wg = eig_ref.shape
    n_seq = out_ref.shape[1]
    share = wa // n_seq
    dot = functools.partial(
        lax.dot_general,
        precision=lax.Precision.HIGHEST,
        preferred_element_type=jnp.float32,
    )
    for a in range(wa):
        rows_ref[a * count : (a + 1) * count, :] = q_ref[:, a * wg : (a + 1) * wg]
    grid = jnp.concatenate(
        [rows_ref[pl.ds(n, wa, stride=count), :] for n in range(count)], axis=0
    )
    ba, bg = ba_ref[...], bg_ref[...]
    scale = eig_ref[...] + damping
    half = dot(grid, bg, NN)
    back = []
    for n in range(count):
        rotated = dot(ba, half[n * wa : (n + 1) * wa], TN)
        back.append(dot(ba, rotated / scale, NN))
    white = dot(jnp.concatenate(back, axis=0), bg, NT).astype(jnp.bfloat16)
    for n in range(count):
        for s in range(n_seq):
            lo = n * wa + s * share
            block = white[lo : lo + share]
            for o in range(out_ref.shape[0]):
                out_ref[o, s, n] = block


def docs_kernel(
    steps,
    span_hbm,
    owner_hbm,
    length_hbm,
    act_hbm,
    grad_hbm,
    pin_hbm,
    pout_hbm,
    after_hbm,
    out_ref,
    act,
    grad,
    pin,
    pout,
    span_ref,
    owner_ref,
    length_ref,
    sems,
    small_sems,
):
    rows, width = act_hbm.shape
    part = width // steps
    wa = pin_hbm.shape[0]
    n_docs = owner_ref.shape[1]
    n_seq, share, wg = out_ref.shape[1:]
    copies = []
    for k in range(steps):
        cols = pl.ds(k * part, part)
        step = []
        for i, (src, dst) in enumerate(
            ((pin_hbm, pin), (act_hbm, act), (pout_hbm, pout), (grad_hbm, grad))
        ):
            copy = pltpu.make_async_copy(src.at[:, cols], dst.at[k], sems.at[k, i])
            copy.start()
            step.append(copy)
        copies.append(step)
    small = []
    for i, (src, dst) in enumerate(
        ((span_hbm, span_ref), (owner_hbm, owner_ref), (length_hbm, length_ref))
    ):
        copy = pltpu.make_async_copy(src, dst, small_sems.at[i])
        copy.start()
        small.append(copy)
    a_sum = jnp.zeros((rows, wa), jnp.float32)
    g_sum = jnp.zeros((rows, wg), jnp.float32)
    for k in range(steps):
        copies[k][0].wait()
        copies[k][1].wait()
        a_sum += lax.dot_general(
            act[k], pin[k], NT, preferred_element_type=jnp.float32
        )
        copies[k][2].wait()
        copies[k][3].wait()
        g_sum += lax.dot_general(
            grad[k], pout[k], NT, preferred_element_type=jnp.float32
        )
    for copy in small:
        copy.wait()
    a_t = a_sum.T.astype(jnp.bfloat16).astype(jnp.float32)
    g_part = g_sum.astype(jnp.bfloat16)
    me = lax.axis_index("seq")
    position = lax.broadcasted_iota(jnp.int32, (wa, rows), 1)
    start = jnp.int32(0)
    spread = []
    for d in range(n_docs):
        end = start + span_ref[0, me, d]
        inside = (position >= start) & (position < end)
        spread.append(jnp.where(inside, a_t, 0.0).astype(jnp.bfloat16))
        start = end
    sums = jnp.dot(
        jnp.concatenate(spread, axis=0), g_part, preferred_element_type=jnp.float32
    )
    out_ref[...] = jnp.zeros_like(out_ref)
    for d in range(n_docs):
        length = jnp.full((wa, wg), length_ref[0, d], jnp.int32).astype(jnp.float32)
        doc = (sums[d * wa : (d + 1) * wa] / length).astype(jnp.bfloat16)
        out_ref[owner_ref[0, d]] = doc.reshape(n_seq, share, wg)


def score_kernel(docs_ref, white_ref, *refs):
    out_refs, sum_ref = refs[:-1], refs[-1]
    n_dp, n_seq, share, wg = docs_ref.shape
    count = white_ref.shape[0]
    n_out = out_refs[0].shape[1]
    width = n_dp * share
    total = docs_ref[:, 0].astype(jnp.float32)
    for s in range(1, n_seq):
        total += docs_ref[:, s].astype(jnp.float32)
    docs = total.reshape(width, wg).astype(jnp.bfloat16)
    white = white_ref[...].reshape(count * share, wg)
    cross = lax.dot_general(white, docs, NT, preferred_element_type=jnp.float32)
    cross = cross.reshape(count, share, width)
    row = lax.broadcasted_iota(jnp.int32, (share, width), 0)
    col = lax.broadcasted_iota(jnp.int32, (share, width), 1)
    same = (row == col % share)[None]
    sum_ref[...] = jnp.sum(jnp.where(same, cross, 0.0), axis=1)
    owner = lax.broadcasted_iota(jnp.int32, (n_dp, width), 0)
    lane = lax.broadcasted_iota(jnp.int32, (n_dp, width), 1)
    gather = (lane // share == owner).astype(jnp.float32)
    me = lax.axis_index("seq")
    for k in range(n_seq):
        block = sum_ref[pl.ds((me ^ k) * n_out, n_out), :]
        out_refs[k][...] = lax.dot_general(
            gather,
            block,
            NT,
            precision=lax.Precision.HIGHEST,
            preferred_element_type=jnp.float32,
        )


def split_dot(x, w):
    bf16 = jnp.bfloat16
    x_hi, w_hi = x.astype(bf16), w.astype(bf16)
    x_lo = (x - x_hi.astype(jnp.float32)).astype(bf16)
    w_lo = (w - w_hi.astype(jnp.float32)).astype(bf16)
    return jnp.dot(
        jnp.concatenate([x_hi, x_lo, x_hi], axis=1),
        jnp.concatenate([w_hi, w_hi, w_lo], axis=0),
        preferred_element_type=jnp.float32,
    )


def side_by_side(x, count):
    rows = x.shape[0] // count
    return jnp.concatenate(
        [x[n * rows : (n + 1) * rows] for n in range(count)], axis=1
    )


def features_kernel(steps, *refs):
    hbm_refs, out_ref, local_refs = refs[:11], refs[11], refs[12:23]
    rows_ref, a_sum, g_sum, blocks, small_sems, sems = refs[23:]
    q, ba_ref, bg_ref, eig_ref, span, owner, length, act, grad, pin, pout = local_refs
    bf16, f32 = jnp.bfloat16, jnp.float32
    count = q.shape[0]
    wa, wg = eig_ref.shape
    rows, part = act.shape[1:]
    n_docs = owner.shape[1]
    n_dev = out_ref.shape[0]
    share = wa // n_dev
    dot = functools.partial(lax.dot_general, preferred_element_type=f32)

    def chunk(k):
        cols = pl.ds(pl.multiple_of(k * part, part), part)
        return [
            pltpu.make_async_copy(
                hbm_refs[7 + i].at[:, cols], local_refs[7 + i].at[k], sems.at[k, i]
            )
            for i in (2, 0, 3, 1)
        ]

    small = []
    for i in range(7):
        copy = pltpu.make_async_copy(hbm_refs[i], local_refs[i], small_sems.at[i])
        copy.start()
        small.append(copy)
    for copy in chunk(0):
        copy.start()
    a_sum[...] = jnp.zeros_like(a_sum)
    g_sum[...] = jnp.zeros_like(g_sum)
    def whiten():
        for copy in small[:4]:
            copy.wait()
        for k in range(1, steps):
            for copy in chunk(k):
                copy.start()
        for a in range(wa):
            rows_ref[a * count : (a + 1) * count, :] = q[:, a * wg : (a + 1) * wg]
        grid = jnp.concatenate(
            [rows_ref[pl.ds(n, wa, stride=count), :] for n in range(count)], axis=0
        )
        ba, bg = ba_ref[...], bg_ref[...]
        scale = jnp.concatenate([eig_ref[...] + damping] * count, axis=1)
        rotated = split_dot(ba.T, side_by_side(split_dot(grid, bg), count))
        back = split_dot(ba, rotated / scale)
        back = jnp.concatenate(
            [back[:, n * wg : (n + 1) * wg] for n in range(count)], axis=0
        )
        white = split_dot(back, bg.T)
        for r in range(share):
            for n in range(count):
                lo = n * wa + r * n_dev
                blocks[share * n_docs + r * count + n] = white[lo : lo + n_dev]

    def add_chunk(k, carry):
        for copy in chunk(k):
            copy.wait()
        a_sum[...] += dot(act[k], pin[k], NT)
        g_sum[...] += dot(grad[k], pout[k], NT)
        return carry

    whiten()
    lax.fori_loop(0, steps, add_chunk, 0)
    for copy in small[4:]:
        copy.wait()
    a_part = a_sum[...].T.astype(bf16).astype(f32)
    g_part = g_sum[...].astype(bf16)
    me = lax.axis_index("seq")
    position = lax.broadcasted_iota(jnp.int32, (wa, rows), 1)
    start = jnp.int32(0)
    spread = []
    for d in range(n_docs):
        end = start + span[0, me, d]
        inside = (position >= start) & (position < end)
        spread.append(jnp.where(inside, a_part, 0.0).astype(bf16))
        start = end
    sums = dot(jnp.concatenate(spread, axis=0), g_part, NN)
    for d in range(n_docs):
        tokens = jnp.full((n_dev, wg), length[0, d], jnp.int32).astype(f32)
        for r in range(share):
            lo = d * wa + r * n_dev
            blocks[r * n_docs + d] = sums[lo : lo + n_dev] / tokens
        target = jnp.full((n_dev, wg), owner[0, d], jnp.int32).astype(f32)
        blocks[share * (n_docs + count) + d] = target
    table = jnp.swapaxes(blocks[...], 0, 1)
    for i in range(out_ref.shape[1]):
        out_ref[:, i] = table[:, i * n_docs : (i + 1) * n_docs].astype(bf16)


def partial_kernel(block_ref, out_ref, rows_ref):
    bf16, f32 = jnp.bfloat16, jnp.float32
    n_dp, n_seq, n_hi = out_ref.shape[:3]
    n_dev, groups, n_docs, wg = block_ref.shape
    share = groups // 2
    count = n_docs
    n_out = n_dev * count // n_seq
    n_lo = n_dp // n_hi
    docs, white = [], []
    for r in range(share):
        part = block_ref[:, r].astype(f32).reshape(n_dp, n_seq, n_docs, wg)
        total = part[:, 0]
        for s in range(1, n_seq):
            total += part[:, s]
        rows_ref[r] = total
        docs.append(
            jnp.concatenate([rows_ref[r, :, d] for d in range(n_docs)], axis=0)
        )
        white.append(block_ref[:, share + r].astype(f32).reshape(n_dev * count, wg))
    rows_ref[share] = (
        block_ref[:, 2 * share].astype(f32).reshape(n_dp, n_seq, n_docs, wg)[:, 0]
    )
    docs = jnp.concatenate(docs, axis=1)
    white = jnp.concatenate(white, axis=1).astype(bf16)
    upper = docs.astype(bf16)
    lower = (docs - upper.astype(f32)).astype(bf16)
    both = lax.dot_general(
        jnp.concatenate([upper, lower], axis=0), white, NT, preferred_element_type=f32
    )
    scores = both[: n_docs * n_dp] + both[n_docs * n_dp :]
    owners = [
        jnp.broadcast_to(rows_ref[share, :, d][:, :1], (n_dp, n_dev * count))
        for d in range(n_docs)
    ]
    routed = []
    for o in range(n_dp):
        row = jnp.zeros((n_dp, n_dev * count), f32)
        for d in range(n_docs):
            mine = owners[d] == float(o)
            row += jnp.where(mine, scores[d * n_dp : (d + 1) * n_dp], 0.0)
        routed.append(row)
    scores = jnp.swapaxes(jnp.stack(routed), 0, 1).reshape(n_dp * n_dp, n_dev * count)
    tall = n_hi * n_dp
    for s in range(n_seq):
        lanes = slice(s * n_out, (s + 1) * n_out)
        packed = jnp.concatenate(
            [scores[lo * tall : (lo + 1) * tall, lanes] for lo in range(n_lo)], axis=1
        )
        for hi in range(n_hi):
            out_ref[:, s, hi, :] = packed[hi * n_dp : (hi + 1) * n_dp]


def finish_kernel(parts_ref, out_ref):
    n_hi = parts_ref.shape[1]
    n_dp, n_out = out_ref.shape
    total = jnp.sum(parts_ref[...], axis=0)
    for lo in range(n_dp // n_hi):
        out_ref[lo * n_hi : (lo + 1) * n_hi, :] = total[:, lo * n_out : (lo + 1) * n_out]


def by_features(
    activations,
    out_grads,
    proj_in,
    proj_out,
    queries,
    basis_a,
    basis_g,
    eigen,
    spans,
    doc_owner,
    doc_lengths,
):
    n_dp, n_seq = lax.axis_size("dp"), lax.axis_size("seq")
    n_dev = n_dp * n_seq
    wa, wg = eigen.shape
    count = queries.shape[0]
    share = wa // n_dev
    n_docs = doc_owner.shape[1]
    height = share * (n_docs + count) + n_docs
    n_out = n_dev * count // n_seq
    n_hi = n_dp * n_out // 128
    bf16, f32 = jnp.bfloat16, jnp.float32
    steps = 5
    part = activations.shape[1] // steps
    params = pltpu.CompilerParams(vmem_limit_bytes=vmem_bytes)
    vmem = pl.BlockSpec(memory_space=pltpu.VMEM)
    hbm = pl.BlockSpec(memory_space=pltpu.HBM)
    small = (queries, basis_a, basis_g, eigen)
    integers = (spans, doc_owner, doc_lengths)
    large = (activations, out_grads, proj_in, proj_out)
    copied = (
        [pltpu.VMEM(x.shape, x.dtype) for x in small]
        + [pltpu.SMEM(x.shape, x.dtype) for x in integers]
        + [pltpu.VMEM((steps, x.shape[0], part), x.dtype) for x in large]
    )
    blocks = pl.pallas_call(
        functools.partial(features_kernel, steps),
        out_shape=jax.ShapeDtypeStruct((n_dev, height // n_docs, n_docs, wg), bf16),
        in_specs=[hbm] * 11,
        out_specs=vmem,
        scratch_shapes=copied
        + [
            pltpu.VMEM((wa * count, wg), f32),
            pltpu.VMEM((activations.shape[0], wa), f32),
            pltpu.VMEM((activations.shape[0], wg), f32),
            pltpu.VMEM((height, n_dev, wg), f32),
            pltpu.SemaphoreType.DMA((7,)),
            pltpu.SemaphoreType.DMA((steps, 4)),
        ],
        compiler_params=params,
        name="features",
    )(*small, *integers, *large)
    everywhere = functools.partial(
        lax.all_to_all,
        axis_name=("dp", "seq"),
        split_axis=0,
        concat_axis=0,
        tiled=True,
    )
    blocks = everywhere(blocks)
    parts = pl.pallas_call(
        partial_kernel,
        out_shape=jax.ShapeDtypeStruct((n_dp, n_seq, n_hi, 128), f32),
        in_specs=[vmem],
        out_specs=vmem,
        scratch_shapes=[pltpu.VMEM((share + 1, n_dp, n_docs, wg), f32)],
        compiler_params=pltpu.CompilerParams(vmem_limit_bytes=small_bytes),
        name="partial",
    )(blocks)
    parts = everywhere(parts.reshape(n_dev, n_hi, 128))
    result = pl.pallas_call(
        finish_kernel,
        out_shape=jax.ShapeDtypeStruct((n_dp, n_out), f32),
        in_specs=[vmem],
        out_specs=vmem,
        compiler_params=pltpu.CompilerParams(vmem_limit_bytes=small_bytes),
        name="finish",
    )(parts)
    return result[None]


def by_rows(
    activations,
    out_grads,
    proj_in,
    proj_out,
    queries,
    basis_a,
    basis_g,
    eigen,
    spans,
    doc_owner,
    doc_lengths,
):
    n_dp, n_seq = lax.axis_size("dp"), lax.axis_size("seq")
    n_dev = n_dp * n_seq
    rows, width = activations.shape
    wa, wg = eigen.shape
    count = queries.shape[0]
    share = wa // n_seq
    steps = 5
    part = width // steps
    bf16, f32 = jnp.bfloat16, jnp.float32
    params = pltpu.CompilerParams(vmem_limit_bytes=vmem_bytes)
    vmem = pl.BlockSpec(memory_space=pltpu.VMEM)
    hbm = pl.BlockSpec(memory_space=pltpu.HBM)

    outgoing = pl.pallas_call(
        whiten_kernel,
        out_shape=jax.ShapeDtypeStruct((n_dp, n_seq, count, share, wg), bf16),
        in_specs=[vmem] * 4,
        out_specs=vmem,
        scratch_shapes=[pltpu.VMEM((wa * count, wg), f32)],
        compiler_params=params,
        name="whiten",
    )(queries, basis_a, basis_g, eigen)
    white = lax.all_to_all(
        outgoing.reshape(n_dev, count, share, wg),
        ("dp", "seq"),
        split_axis=0,
        concat_axis=0,
        tiled=True,
    )

    docs = pl.pallas_call(
        functools.partial(docs_kernel, steps),
        out_shape=jax.ShapeDtypeStruct((n_dp, n_seq, share, wg), bf16),
        in_specs=[hbm] * 8,
        out_specs=vmem,
        scratch_shapes=[
            pltpu.VMEM((steps, rows, part), bf16),
            pltpu.VMEM((steps, rows, part), bf16),
            pltpu.VMEM((steps, wa, part), bf16),
            pltpu.VMEM((steps, wg, part), bf16),
            pltpu.SMEM(spans.shape, jnp.int32),
            pltpu.SMEM(doc_owner.shape, jnp.int32),
            pltpu.SMEM(doc_lengths.shape, jnp.int32),
            pltpu.SemaphoreType.DMA((steps, 4)),
            pltpu.SemaphoreType.DMA((3,)),
        ],
        compiler_params=params,
        name="docs",
    )(
        spans,
        doc_owner,
        doc_lengths,
        activations,
        out_grads,
        proj_in,
        proj_out,
        outgoing,
    )
    docs = lax.all_to_all(
        docs.reshape(n_dev, share, wg),
        ("dp", "seq"),
        split_axis=0,
        concat_axis=0,
        tiled=True,
    )

    n_query = n_dev * count
    n_out = n_query // n_seq
    parts = pl.pallas_call(
        score_kernel,
        out_shape=[jax.ShapeDtypeStruct((n_dp, n_out), f32)] * n_seq,
        in_specs=[vmem] * 2,
        out_specs=[vmem] * n_seq,
        scratch_shapes=[pltpu.VMEM((n_query, n_dp * share), f32)],
        compiler_params=params,
        name="score",
    )(docs.reshape(n_dp, n_seq, share, wg), white.reshape(n_query, share, wg))
    result = parts[0]
    for k in range(n_seq - 1, 0, -1):
        pairs = [(i, i ^ k) for i in range(n_seq)]
        result = result + lax.ppermute(parts[k], "seq", pairs)
    return result[None]


def per_device(*args):
    n_dp, n_seq = lax.axis_size("dp"), lax.axis_size("seq")
    n_dev = n_dp * n_seq
    wa, wg = args[7].shape
    count = args[4].shape[0]
    share = wa // n_dev
    n_out = n_dp * count
    fits = (
        share * n_dev == wa
        and wg == 128
        and n_dp % 8 == 0
        and n_dp <= 256
        and args[9].shape[1] == count == 4
        and 128 % n_out == 0
        and n_dp * n_out % 128 == 0
    )
    return (by_features if fits else by_rows)(*args)


def solution(mesh):
    return jax.shard_map(
        per_device,
        mesh=mesh,
        in_specs=(
            P(("dp", "seq"), None),
            P(("dp", "seq"), None),
            P(),
            P(),
            P(("dp", "seq"), None),
            P(),
            P(),
            P(),
            P("dp", None, None),
            P("dp", None),
            P("dp", None),
        ),
        out_specs=P("dp", None, "seq"),
        check_vma=False,
    )
```

```python
import functools

import jax
import jax.numpy as jnp
from jax import lax
from jax.experimental import pallas as pl
from jax.experimental.pallas import tpu as pltpu
from jax.sharding import PartitionSpec as P

damping = 0.1
vmem_bytes = 64 * 1024 * 1024
small_bytes = 16 * 1024 * 1024

NT = (((1,), (1,)), ((), ()))
NN = (((1,), (0,)), ((), ()))
TN = (((0,), (0,)), ((), ()))


def whiten_kernel(q_ref, ba_ref, bg_ref, eig_ref, out_ref, rows_ref):
    count = q_ref.shape[0]
    wa, wg = eig_ref.shape
    n_seq = out_ref.shape[1]
    share = wa // n_seq
    dot = functools.partial(
        lax.dot_general,
        precision=lax.Precision.HIGHEST,
        preferred_element_type=jnp.float32,
    )
    for a in range(wa):
        rows_ref[a * count : (a + 1) * count, :] = q_ref[:, a * wg : (a + 1) * wg]
    grid = jnp.concatenate(
        [rows_ref[pl.ds(n, wa, stride=count), :] for n in range(count)], axis=0
    )
    ba, bg = ba_ref[...], bg_ref[...]
    scale = eig_ref[...] + damping
    half = dot(grid, bg, NN)
    back = []
    for n in range(count):
        rotated = dot(ba, half[n * wa : (n + 1) * wa], TN)
        back.append(dot(ba, rotated / scale, NN))
    white = dot(jnp.concatenate(back, axis=0), bg, NT).astype(jnp.bfloat16)
    for n in range(count):
        for s in range(n_seq):
            lo = n * wa + s * share
            block = white[lo : lo + share]
            for o in range(out_ref.shape[0]):
                out_ref[o, s, n] = block


def docs_kernel(
    steps,
    span_hbm,
    owner_hbm,
    length_hbm,
    act_hbm,
    grad_hbm,
    pin_hbm,
    pout_hbm,
    after_hbm,
    out_ref,
    act,
    grad,
    pin,
    pout,
    span_ref,
    owner_ref,
    length_ref,
    sems,
    small_sems,
):
    rows, width = act_hbm.shape
    part = width // steps
    wa = pin_hbm.shape[0]
    n_docs = owner_ref.shape[1]
    n_seq, share, wg = out_ref.shape[1:]
    copies = []
    for k in range(steps):
        cols = pl.ds(k * part, part)
        step = []
        for i, (src, dst) in enumerate(
            ((pin_hbm, pin), (act_hbm, act), (pout_hbm, pout), (grad_hbm, grad))
        ):
            copy = pltpu.make_async_copy(src.at[:, cols], dst.at[k], sems.at[k, i])
            copy.start()
            step.append(copy)
        copies.append(step)
    small = []
    for i, (src, dst) in enumerate(
        ((span_hbm, span_ref), (owner_hbm, owner_ref), (length_hbm, length_ref))
    ):
        copy = pltpu.make_async_copy(src, dst, small_sems.at[i])
        copy.start()
        small.append(copy)
    a_sum = jnp.zeros((rows, wa), jnp.float32)
    g_sum = jnp.zeros((rows, wg), jnp.float32)
    for k in range(steps):
        copies[k][0].wait()
        copies[k][1].wait()
        a_sum += lax.dot_general(
            act[k], pin[k], NT, preferred_element_type=jnp.float32
        )
        copies[k][2].wait()
        copies[k][3].wait()
        g_sum += lax.dot_general(
            grad[k], pout[k], NT, preferred_element_type=jnp.float32
        )
    for copy in small:
        copy.wait()
    a_t = a_sum.T.astype(jnp.bfloat16).astype(jnp.float32)
    g_part = g_sum.astype(jnp.bfloat16)
    me = lax.axis_index("seq")
    position = lax.broadcasted_iota(jnp.int32, (wa, rows), 1)
    start = jnp.int32(0)
    spread = []
    for d in range(n_docs):
        end = start + span_ref[0, me, d]
        inside = (position >= start) & (position < end)
        spread.append(jnp.where(inside, a_t, 0.0).astype(jnp.bfloat16))
        start = end
    sums = jnp.dot(
        jnp.concatenate(spread, axis=0), g_part, preferred_element_type=jnp.float32
    )
    out_ref[...] = jnp.zeros_like(out_ref)
    for d in range(n_docs):
        length = jnp.full((wa, wg), length_ref[0, d], jnp.int32).astype(jnp.float32)
        doc = (sums[d * wa : (d + 1) * wa] / length).astype(jnp.bfloat16)
        out_ref[owner_ref[0, d]] = doc.reshape(n_seq, share, wg)


def score_kernel(docs_ref, white_ref, *refs):
    out_refs, sum_ref = refs[:-1], refs[-1]
    n_dp, n_seq, share, wg = docs_ref.shape
    count = white_ref.shape[0]
    n_out = out_refs[0].shape[1]
    width = n_dp * share
    total = docs_ref[:, 0].astype(jnp.float32)
    for s in range(1, n_seq):
        total += docs_ref[:, s].astype(jnp.float32)
    docs = total.reshape(width, wg).astype(jnp.bfloat16)
    white = white_ref[...].reshape(count * share, wg)
    cross = lax.dot_general(white, docs, NT, preferred_element_type=jnp.float32)
    cross = cross.reshape(count, share, width)
    row = lax.broadcasted_iota(jnp.int32, (share, width), 0)
    col = lax.broadcasted_iota(jnp.int32, (share, width), 1)
    same = (row == col % share)[None]
    sum_ref[...] = jnp.sum(jnp.where(same, cross, 0.0), axis=1)
    owner = lax.broadcasted_iota(jnp.int32, (n_dp, width), 0)
    lane = lax.broadcasted_iota(jnp.int32, (n_dp, width), 1)
    gather = (lane // share == owner).astype(jnp.float32)
    me = lax.axis_index("seq")
    for k in range(n_seq):
        block = sum_ref[pl.ds((me ^ k) * n_out, n_out), :]
        out_refs[k][...] = lax.dot_general(
            gather,
            block,
            NT,
            precision=lax.Precision.HIGHEST,
            preferred_element_type=jnp.float32,
        )


def split_dot(x, w):
    bf16 = jnp.bfloat16
    x_hi, w_hi = x.astype(bf16), w.astype(bf16)
    x_lo = (x - x_hi.astype(jnp.float32)).astype(bf16)
    w_lo = (w - w_hi.astype(jnp.float32)).astype(bf16)
    return jnp.dot(
        jnp.concatenate([x_hi, x_lo, x_hi], axis=1),
        jnp.concatenate([w_hi, w_hi, w_lo], axis=0),
        preferred_element_type=jnp.float32,
    )


def side_by_side(x, count):
    rows = x.shape[0] // count
    return jnp.concatenate(
        [x[n * rows : (n + 1) * rows] for n in range(count)], axis=1
    )


def features_kernel(steps, *refs):
    hbm_refs, out_ref, local_refs = refs[:11], refs[11], refs[12:23]
    rows_ref, a_sum, g_sum, blocks, small_sems, sems = refs[23:]
    q, ba_ref, bg_ref, eig_ref, span, owner, length, act, grad, pin, pout = local_refs
    bf16, f32 = jnp.bfloat16, jnp.float32
    count = q.shape[0]
    wa, wg = eig_ref.shape
    rows, part = act.shape[1:]
    n_docs = owner.shape[1]
    n_dev = out_ref.shape[0]
    share = wa // n_dev
    dot = functools.partial(lax.dot_general, preferred_element_type=f32)

    def chunk(k):
        cols = pl.ds(pl.multiple_of(k * part, part), part)
        return [
            pltpu.make_async_copy(
                hbm_refs[7 + i].at[:, cols], local_refs[7 + i].at[k], sems.at[k, i]
            )
            for i in (2, 0, 3, 1)
        ]

    small = []
    for i in range(7):
        copy = pltpu.make_async_copy(hbm_refs[i], local_refs[i], small_sems.at[i])
        copy.start()
        small.append(copy)
    for k in range(steps):
        for copy in chunk(k):
            copy.start(priority=1)
    a_sum[...] = jnp.zeros_like(a_sum)
    g_sum[...] = jnp.zeros_like(g_sum)
    def whiten():
        for copy in small[:4]:
            copy.wait()
        for a in range(wa):
            rows_ref[a * count : (a + 1) * count, :] = q[:, a * wg : (a + 1) * wg]
        grid = jnp.concatenate(
            [rows_ref[pl.ds(n, wa, stride=count), :] for n in range(count)], axis=0
        )
        ba, bg = ba_ref[...], bg_ref[...]
        scale = jnp.concatenate([eig_ref[...] + damping] * count, axis=1)
        rotated = split_dot(ba.T, side_by_side(split_dot(grid, bg), count))
        back = split_dot(ba, rotated / scale)
        back = jnp.concatenate(
            [back[:, n * wg : (n + 1) * wg] for n in range(count)], axis=0
        )
        white = split_dot(back, bg.T)
        for r in range(share):
            for n in range(count):
                lo = n * wa + r * n_dev
                blocks[(n_docs + n) * share + r] = white[lo : lo + n_dev]

    def add_chunk(k, carry):
        for copy in chunk(k):
            copy.wait()
        a_sum[...] += dot(act[k], pin[k], NT)
        g_sum[...] += dot(grad[k], pout[k], NT)
        return carry

    whiten()
    lax.fori_loop(0, steps, add_chunk, 0)
    for copy in small[4:]:
        copy.wait()
    a_part = a_sum[...].T.astype(bf16).astype(f32)
    g_part = g_sum[...].astype(bf16)
    me = lax.axis_index("seq")
    position = lax.broadcasted_iota(jnp.int32, (wa, rows), 1)
    start = jnp.int32(0)
    spread = []
    for d in range(n_docs):
        end = start + span[0, me, d]
        inside = (position >= start) & (position < end)
        spread.append(jnp.where(inside, a_part, 0.0).astype(bf16))
        start = end
    sums = dot(jnp.concatenate(spread, axis=0), g_part, NN)
    for d in range(n_docs):
        tokens = jnp.full((n_dev, wg), length[0, d], jnp.int32).astype(f32)
        for r in range(share):
            lo = d * wa + r * n_dev
            blocks[d * share + r] = sums[lo : lo + n_dev] / tokens
    lane = lax.broadcasted_iota(jnp.int32, (n_dev, wg), 1)
    each = n_docs // share
    for r in range(share):
        target = jnp.full((n_dev, wg), owner[0, r * each], jnp.int32)
        for i in range(1, each):
            target = jnp.where(lane >= i * (wg // each), owner[0, r * each + i], target)
        blocks[(n_docs + count) * share + r] = target.astype(f32)
    table = jnp.swapaxes(blocks[...], 0, 1)
    for i in range(out_ref.shape[1]):
        out_ref[:, i] = table[:, i * share : (i + 1) * share].astype(bf16)


def partial_kernel(n_docs, block_ref, out_ref, rows_ref, white_ref):
    bf16, f32 = jnp.bfloat16, jnp.float32
    n_dp, n_seq, n_hi = out_ref.shape[:3]
    n_dev, slots, share, wg = block_ref.shape
    count = slots - n_docs - 1
    n_out = n_dev * count // n_seq
    n_lo = n_dp // n_hi
    docs = []
    for d in range(n_docs):
        part = block_ref[:, d].astype(f32).reshape(n_dp, n_seq, share, wg)
        total = part[:, 0]
        for s in range(1, n_seq):
            total += part[:, s]
        rows_ref[:n_dp] = total
        docs.append(
            jnp.concatenate([rows_ref[:n_dp, r] for r in range(share)], axis=1)
        )
    docs = jnp.concatenate(docs, axis=0)
    for n in range(count):
        rows_ref[...] = block_ref[:, n_docs + n].astype(f32)
        for r in range(share):
            white_ref[r, pl.ds(n, n_dev, stride=count), :] = rows_ref[:, r]
    white = jnp.concatenate([white_ref[r] for r in range(share)], axis=1).astype(bf16)
    part = block_ref[:, n_docs + count].astype(f32)
    rows_ref[:n_dp] = part.reshape(n_dp, n_seq, share, wg)[:, 0]
    each = n_docs // share
    owners = []
    for d in range(n_docs):
        lane = d % each * (wg // each)
        column = rows_ref[:n_dp, d // each][:, lane : lane + 1]
        owners.append(jnp.broadcast_to(column, (n_dp, n_dev * count)))
    upper = docs.astype(bf16)
    lower = (docs - upper.astype(f32)).astype(bf16)
    both = lax.dot_general(
        jnp.concatenate([upper, lower], axis=0), white, NT, preferred_element_type=f32
    )
    scores = both[: n_docs * n_dp] + both[n_docs * n_dp :]
    routed = []
    for o in range(n_dp):
        row = jnp.zeros((n_dp, n_dev * count), f32)
        for d in range(n_docs):
            mine = owners[d] == float(o)
            row += jnp.where(mine, scores[d * n_dp : (d + 1) * n_dp], 0.0)
        routed.append(row)
    scores = jnp.swapaxes(jnp.stack(routed), 0, 1).reshape(n_dp * n_dp, n_dev * count)
    tall = n_hi * n_dp
    for s in range(n_seq):
        lanes = slice(s * n_out, (s + 1) * n_out)
        packed = jnp.concatenate(
            [scores[lo * tall : (lo + 1) * tall, lanes] for lo in range(n_lo)], axis=1
        )
        for hi in range(n_hi):
            out_ref[:, s, hi, :] = packed[hi * n_dp : (hi + 1) * n_dp]


def finish_kernel(parts_ref, out_ref):
    n_hi = parts_ref.shape[1]
    n_dp, n_out = out_ref.shape
    total = jnp.sum(parts_ref[...], axis=0)
    for lo in range(n_dp // n_hi):
        out_ref[lo * n_hi : (lo + 1) * n_hi, :] = total[:, lo * n_out : (lo + 1) * n_out]


def by_features(
    activations,
    out_grads,
    proj_in,
    proj_out,
    queries,
    basis_a,
    basis_g,
    eigen,
    spans,
    doc_owner,
    doc_lengths,
):
    n_dp, n_seq = lax.axis_size("dp"), lax.axis_size("seq")
    n_dev = n_dp * n_seq
    wa, wg = eigen.shape
    count = queries.shape[0]
    share = wa // n_dev
    n_docs = doc_owner.shape[1]
    height = share * (n_docs + count + 1)
    n_out = n_dev * count // n_seq
    n_hi = n_dp * n_out // 128
    bf16, f32 = jnp.bfloat16, jnp.float32
    steps = 5
    part = activations.shape[1] // steps
    params = pltpu.CompilerParams(vmem_limit_bytes=vmem_bytes)
    vmem = pl.BlockSpec(memory_space=pltpu.VMEM)
    hbm = pl.BlockSpec(memory_space=pltpu.HBM)
    small = (queries, basis_a, basis_g, eigen)
    integers = (spans, doc_owner, doc_lengths)
    large = (activations, out_grads, proj_in, proj_out)
    copied = (
        [pltpu.VMEM(x.shape, x.dtype) for x in small]
        + [pltpu.SMEM(x.shape, x.dtype) for x in integers]
        + [pltpu.VMEM((steps, x.shape[0], part), x.dtype) for x in large]
    )
    blocks = pl.pallas_call(
        functools.partial(features_kernel, steps),
        out_shape=jax.ShapeDtypeStruct((n_dev, height // share, share, wg), bf16),
        in_specs=[hbm] * 11,
        out_specs=vmem,
        scratch_shapes=copied
        + [
            pltpu.VMEM((wa * count, wg), f32),
            pltpu.VMEM((activations.shape[0], wa), f32),
            pltpu.VMEM((activations.shape[0], wg), f32),
            pltpu.VMEM((height, n_dev, wg), f32),
            pltpu.SemaphoreType.DMA((7,)),
            pltpu.SemaphoreType.DMA((steps, 4)),
        ],
        compiler_params=params,
        name="features",
    )(*small, *integers, *large)
    everywhere = functools.partial(
        lax.all_to_all,
        axis_name=("dp", "seq"),
        split_axis=0,
        concat_axis=0,
        tiled=True,
    )
    blocks = everywhere(blocks)
    parts = pl.pallas_call(
        functools.partial(partial_kernel, n_docs),
        out_shape=jax.ShapeDtypeStruct((n_dp, n_seq, n_hi, 128), f32),
        in_specs=[vmem],
        out_specs=vmem,
        scratch_shapes=[
            pltpu.VMEM((n_dev, share, wg), f32),
            pltpu.VMEM((share, n_dev * count, wg), f32),
        ],
        compiler_params=pltpu.CompilerParams(vmem_limit_bytes=small_bytes),
        name="partial",
    )(blocks)
    parts = everywhere(parts.reshape(n_dev, n_hi, 128))
    result = pl.pallas_call(
        finish_kernel,
        out_shape=jax.ShapeDtypeStruct((n_dp, n_out), f32),
        in_specs=[vmem],
        out_specs=vmem,
        compiler_params=pltpu.CompilerParams(vmem_limit_bytes=small_bytes),
        name="finish",
    )(parts)
    return result[None]


def by_rows(
    activations,
    out_grads,
    proj_in,
    proj_out,
    queries,
    basis_a,
    basis_g,
    eigen,
    spans,
    doc_owner,
    doc_lengths,
):
    n_dp, n_seq = lax.axis_size("dp"), lax.axis_size("seq")
    n_dev = n_dp * n_seq
    rows, width = activations.shape
    wa, wg = eigen.shape
    count = queries.shape[0]
    share = wa // n_seq
    steps = 5
    part = width // steps
    bf16, f32 = jnp.bfloat16, jnp.float32
    params = pltpu.CompilerParams(vmem_limit_bytes=vmem_bytes)
    vmem = pl.BlockSpec(memory_space=pltpu.VMEM)
    hbm = pl.BlockSpec(memory_space=pltpu.HBM)

    outgoing = pl.pallas_call(
        whiten_kernel,
        out_shape=jax.ShapeDtypeStruct((n_dp, n_seq, count, share, wg), bf16),
        in_specs=[vmem] * 4,
        out_specs=vmem,
        scratch_shapes=[pltpu.VMEM((wa * count, wg), f32)],
        compiler_params=params,
        name="whiten",
    )(queries, basis_a, basis_g, eigen)
    white = lax.all_to_all(
        outgoing.reshape(n_dev, count, share, wg),
        ("dp", "seq"),
        split_axis=0,
        concat_axis=0,
        tiled=True,
    )

    docs = pl.pallas_call(
        functools.partial(docs_kernel, steps),
        out_shape=jax.ShapeDtypeStruct((n_dp, n_seq, share, wg), bf16),
        in_specs=[hbm] * 8,
        out_specs=vmem,
        scratch_shapes=[
            pltpu.VMEM((steps, rows, part), bf16),
            pltpu.VMEM((steps, rows, part), bf16),
            pltpu.VMEM((steps, wa, part), bf16),
            pltpu.VMEM((steps, wg, part), bf16),
            pltpu.SMEM(spans.shape, jnp.int32),
            pltpu.SMEM(doc_owner.shape, jnp.int32),
            pltpu.SMEM(doc_lengths.shape, jnp.int32),
            pltpu.SemaphoreType.DMA((steps, 4)),
            pltpu.SemaphoreType.DMA((3,)),
        ],
        compiler_params=params,
        name="docs",
    )(
        spans,
        doc_owner,
        doc_lengths,
        activations,
        out_grads,
        proj_in,
        proj_out,
        outgoing,
    )
    docs = lax.all_to_all(
        docs.reshape(n_dev, share, wg),
        ("dp", "seq"),
        split_axis=0,
        concat_axis=0,
        tiled=True,
    )

    n_query = n_dev * count
    n_out = n_query // n_seq
    parts = pl.pallas_call(
        score_kernel,
        out_shape=[jax.ShapeDtypeStruct((n_dp, n_out), f32)] * n_seq,
        in_specs=[vmem] * 2,
        out_specs=[vmem] * n_seq,
        scratch_shapes=[pltpu.VMEM((n_query, n_dp * share), f32)],
        compiler_params=params,
        name="score",
    )(docs.reshape(n_dp, n_seq, share, wg), white.reshape(n_query, share, wg))
    result = parts[0]
    for k in range(n_seq - 1, 0, -1):
        pairs = [(i, i ^ k) for i in range(n_seq)]
        result = result + lax.ppermute(parts[k], "seq", pairs)
    return result[None]


def per_device(*args):
    n_dp, n_seq = lax.axis_size("dp"), lax.axis_size("seq")
    n_dev = n_dp * n_seq
    wa, wg = args[7].shape
    count = args[4].shape[0]
    share = wa // n_dev
    n_out = n_dp * count
    fits = (
        share > 0
        and share * n_dev == wa
        and wg == 128
        and n_dp % 8 == 0
        and n_dp <= 256
        and args[9].shape[1] % share == 0
        and 128 % n_out == 0
        and n_dp * n_out % 128 == 0
    )
    return (by_features if fits else by_rows)(*args)


def solution(mesh):
    return jax.shard_map(
        per_device,
        mesh=mesh,
        in_specs=(
            P(("dp", "seq"), None),
            P(("dp", "seq"), None),
            P(),
            P(),
            P(("dp", "seq"), None),
            P(),
            P(),
            P(),
            P("dp", None, None),
            P("dp", None),
            P("dp", None),
        ),
        out_specs=P("dp", None, "seq"),
        check_vma=False,
    )
```

```python
import functools

import jax
import jax.numpy as jnp
from jax import lax
from jax.experimental import pallas as pl
from jax.experimental.pallas import tpu as pltpu
from jax.sharding import PartitionSpec as P

damping = 0.1
vmem_bytes = 64 * 1024 * 1024
features_bytes = 32 * 1024 * 1024
small_bytes = 16 * 1024 * 1024

NT = (((1,), (1,)), ((), ()))
NN = (((1,), (0,)), ((), ()))
TN = (((0,), (0,)), ((), ()))


def whiten_kernel(q_ref, ba_ref, bg_ref, eig_ref, out_ref, rows_ref):
    count = q_ref.shape[0]
    wa, wg = eig_ref.shape
    n_seq = out_ref.shape[1]
    share = wa // n_seq
    dot = functools.partial(
        lax.dot_general,
        precision=lax.Precision.HIGHEST,
        preferred_element_type=jnp.float32,
    )
    for a in range(wa):
        rows_ref[a * count : (a + 1) * count, :] = q_ref[:, a * wg : (a + 1) * wg]
    grid = jnp.concatenate(
        [rows_ref[pl.ds(n, wa, stride=count), :] for n in range(count)], axis=0
    )
    ba, bg = ba_ref[...], bg_ref[...]
    scale = eig_ref[...] + damping
    half = dot(grid, bg, NN)
    back = []
    for n in range(count):
        rotated = dot(ba, half[n * wa : (n + 1) * wa], TN)
        back.append(dot(ba, rotated / scale, NN))
    white = dot(jnp.concatenate(back, axis=0), bg, NT).astype(jnp.bfloat16)
    for n in range(count):
        for s in range(n_seq):
            lo = n * wa + s * share
            block = white[lo : lo + share]
            for o in range(out_ref.shape[0]):
                out_ref[o, s, n] = block


def docs_kernel(
    steps,
    span_hbm,
    owner_hbm,
    length_hbm,
    act_hbm,
    grad_hbm,
    pin_hbm,
    pout_hbm,
    after_hbm,
    out_ref,
    act,
    grad,
    pin,
    pout,
    span_ref,
    owner_ref,
    length_ref,
    sems,
    small_sems,
):
    rows, width = act_hbm.shape
    part = width // steps
    wa = pin_hbm.shape[0]
    n_docs = owner_ref.shape[1]
    n_seq, share, wg = out_ref.shape[1:]
    copies = []
    for k in range(steps):
        cols = pl.ds(k * part, part)
        step = []
        for i, (src, dst) in enumerate(
            ((pin_hbm, pin), (act_hbm, act), (pout_hbm, pout), (grad_hbm, grad))
        ):
            copy = pltpu.make_async_copy(src.at[:, cols], dst.at[k], sems.at[k, i])
            copy.start()
            step.append(copy)
        copies.append(step)
    small = []
    for i, (src, dst) in enumerate(
        ((span_hbm, span_ref), (owner_hbm, owner_ref), (length_hbm, length_ref))
    ):
        copy = pltpu.make_async_copy(src, dst, small_sems.at[i])
        copy.start()
        small.append(copy)
    a_sum = jnp.zeros((rows, wa), jnp.float32)
    g_sum = jnp.zeros((rows, wg), jnp.float32)
    for k in range(steps):
        copies[k][0].wait()
        copies[k][1].wait()
        a_sum += lax.dot_general(
            act[k], pin[k], NT, preferred_element_type=jnp.float32
        )
        copies[k][2].wait()
        copies[k][3].wait()
        g_sum += lax.dot_general(
            grad[k], pout[k], NT, preferred_element_type=jnp.float32
        )
    for copy in small:
        copy.wait()
    a_t = a_sum.T.astype(jnp.bfloat16).astype(jnp.float32)
    g_part = g_sum.astype(jnp.bfloat16)
    me = lax.axis_index("seq")
    position = lax.broadcasted_iota(jnp.int32, (wa, rows), 1)
    start = jnp.int32(0)
    spread = []
    for d in range(n_docs):
        end = start + span_ref[0, me, d]
        inside = (position >= start) & (position < end)
        spread.append(jnp.where(inside, a_t, 0.0).astype(jnp.bfloat16))
        start = end
    sums = jnp.dot(
        jnp.concatenate(spread, axis=0), g_part, preferred_element_type=jnp.float32
    )
    out_ref[...] = jnp.zeros_like(out_ref)
    for d in range(n_docs):
        length = jnp.full((wa, wg), length_ref[0, d], jnp.int32).astype(jnp.float32)
        doc = (sums[d * wa : (d + 1) * wa] / length).astype(jnp.bfloat16)
        out_ref[owner_ref[0, d]] = doc.reshape(n_seq, share, wg)


def score_kernel(docs_ref, white_ref, *refs):
    out_refs, sum_ref = refs[:-1], refs[-1]
    n_dp, n_seq, share, wg = docs_ref.shape
    count = white_ref.shape[0]
    n_out = out_refs[0].shape[1]
    width = n_dp * share
    total = docs_ref[:, 0].astype(jnp.float32)
    for s in range(1, n_seq):
        total += docs_ref[:, s].astype(jnp.float32)
    docs = total.reshape(width, wg).astype(jnp.bfloat16)
    white = white_ref[...].reshape(count * share, wg)
    cross = lax.dot_general(white, docs, NT, preferred_element_type=jnp.float32)
    cross = cross.reshape(count, share, width)
    row = lax.broadcasted_iota(jnp.int32, (share, width), 0)
    col = lax.broadcasted_iota(jnp.int32, (share, width), 1)
    same = (row == col % share)[None]
    sum_ref[...] = jnp.sum(jnp.where(same, cross, 0.0), axis=1)
    owner = lax.broadcasted_iota(jnp.int32, (n_dp, width), 0)
    lane = lax.broadcasted_iota(jnp.int32, (n_dp, width), 1)
    gather = (lane // share == owner).astype(jnp.float32)
    me = lax.axis_index("seq")
    for k in range(n_seq):
        block = sum_ref[pl.ds((me ^ k) * n_out, n_out), :]
        out_refs[k][...] = lax.dot_general(
            gather,
            block,
            NT,
            precision=lax.Precision.HIGHEST,
            preferred_element_type=jnp.float32,
        )


def split_dot(x, w):
    bf16 = jnp.bfloat16
    x_hi, w_hi = x.astype(bf16), w.astype(bf16)
    x_lo = (x - x_hi.astype(jnp.float32)).astype(bf16)
    w_lo = (w - w_hi.astype(jnp.float32)).astype(bf16)
    return jnp.dot(
        jnp.concatenate([x_hi, x_lo, x_hi], axis=1),
        jnp.concatenate([w_hi, w_hi, w_lo], axis=0),
        preferred_element_type=jnp.float32,
    )


def side_by_side(x, count):
    rows = x.shape[0] // count
    return jnp.concatenate(
        [x[n * rows : (n + 1) * rows] for n in range(count)], axis=1
    )


def features_kernel(steps, *refs):
    hbm_refs, out_ref, local_refs = refs[:11], refs[11], refs[12:23]
    rows_ref, a_sum, g_sum, blocks, small_sems, sems = refs[23:]
    q, ba_ref, bg_ref, eig_ref, span, owner, length, act, grad, pin, pout = local_refs
    bf16, f32 = jnp.bfloat16, jnp.float32
    count = q.shape[0]
    wa, wg = eig_ref.shape
    rows, part = act.shape[1:]
    n_docs = owner.shape[1]
    n_dev = out_ref.shape[0]
    share = wa // n_dev
    dot = functools.partial(lax.dot_general, preferred_element_type=f32)

    def chunk(k):
        cols = pl.ds(pl.multiple_of(k * part, part), part)
        return [
            pltpu.make_async_copy(
                hbm_refs[7 + i].at[:, cols], local_refs[7 + i].at[k], sems.at[k, i]
            )
            for i in (2, 0, 3, 1)
        ]

    small = []
    for i in range(7):
        copy = pltpu.make_async_copy(hbm_refs[i], local_refs[i], small_sems.at[i])
        copy.start()
        small.append(copy)
    for k in range(steps):
        for copy in chunk(k):
            copy.start(priority=1)
    a_sum[...] = jnp.zeros_like(a_sum)
    g_sum[...] = jnp.zeros_like(g_sum)
    def whiten():
        for copy in small[:4]:
            copy.wait()
        for a in range(wa):
            rows_ref[a * count : (a + 1) * count, :] = q[:, a * wg : (a + 1) * wg]
        grid = jnp.concatenate(
            [rows_ref[pl.ds(n, wa, stride=count), :] for n in range(count)], axis=0
        )
        ba, bg = ba_ref[...], bg_ref[...]
        scale = jnp.concatenate([eig_ref[...] + damping] * count, axis=1)
        rotated = split_dot(ba.T, side_by_side(split_dot(grid, bg), count))
        back = split_dot(ba, rotated / scale)
        back = jnp.concatenate(
            [back[:, n * wg : (n + 1) * wg] for n in range(count)], axis=0
        )
        white = split_dot(back, bg.T)
        for r in range(share):
            for n in range(count):
                lo = n * wa + r * n_dev
                blocks[(n_docs + n) * share + r] = white[lo : lo + n_dev]

    def add_chunk(k, carry):
        for copy in chunk(k):
            copy.wait()
        a_sum[...] += dot(act[k], pin[k], NT)
        g_sum[...] += dot(grad[k], pout[k], NT)
        return carry

    whiten()
    lax.fori_loop(0, steps, add_chunk, 0)
    for copy in small[4:]:
        copy.wait()
    a_part = a_sum[...].T.astype(bf16).astype(f32)
    g_part = g_sum[...].astype(bf16)
    me = lax.axis_index("seq")
    position = lax.broadcasted_iota(jnp.int32, (wa, rows), 1)
    start = jnp.int32(0)
    spread = []
    for d in range(n_docs):
        end = start + span[0, me, d]
        inside = (position >= start) & (position < end)
        spread.append(jnp.where(inside, a_part, 0.0).astype(bf16))
        start = end
    sums = dot(jnp.concatenate(spread, axis=0), g_part, NN)
    for d in range(n_docs):
        tokens = jnp.full((n_dev, wg), length[0, d], jnp.int32).astype(f32)
        for r in range(share):
            lo = d * wa + r * n_dev
            blocks[d * share + r] = sums[lo : lo + n_dev] / tokens
    lane = lax.broadcasted_iota(jnp.int32, (n_dev, wg), 1)
    each = n_docs // share
    for r in range(share):
        target = jnp.full((n_dev, wg), owner[0, r * each], jnp.int32)
        for i in range(1, each):
            target = jnp.where(lane >= i * (wg // each), owner[0, r * each + i], target)
        blocks[(n_docs + count) * share + r] = target.astype(f32)
    table = jnp.swapaxes(blocks[...], 0, 1)
    for i in range(out_ref.shape[1]):
        out_ref[:, i] = table[:, i * share : (i + 1) * share].astype(bf16)


def partial_kernel(n_docs, block_ref, out_ref, rows_ref, white_ref):
    bf16, f32 = jnp.bfloat16, jnp.float32
    n_dp, n_seq, n_hi = out_ref.shape[:3]
    n_dev, slots, share, wg = block_ref.shape
    count = slots - n_docs - 1
    n_out = n_dev * count // n_seq
    n_lo = n_dp // n_hi
    docs = []
    for d in range(n_docs):
        part = block_ref[:, d].astype(f32).reshape(n_dp, n_seq, share, wg)
        total = part[:, 0]
        for s in range(1, n_seq):
            total += part[:, s]
        rows_ref[:n_dp] = total
        docs.append(
            jnp.concatenate([rows_ref[:n_dp, r] for r in range(share)], axis=1)
        )
    docs = jnp.concatenate(docs, axis=0)
    for n in range(count):
        rows_ref[...] = block_ref[:, n_docs + n].astype(f32)
        for r in range(share):
            white_ref[r, pl.ds(n, n_dev, stride=count), :] = rows_ref[:, r]
    white = jnp.concatenate([white_ref[r] for r in range(share)], axis=1).astype(bf16)
    part = block_ref[:, n_docs + count].astype(f32)
    rows_ref[:n_dp] = part.reshape(n_dp, n_seq, share, wg)[:, 0]
    each = n_docs // share
    owners = []
    for d in range(n_docs):
        lane = d % each * (wg // each)
        column = rows_ref[:n_dp, d // each][:, lane : lane + 1]
        owners.append(jnp.broadcast_to(column, (n_dp, n_dev * count)))
    upper = docs.astype(bf16)
    lower = (docs - upper.astype(f32)).astype(bf16)
    both = lax.dot_general(
        jnp.concatenate([upper, lower], axis=0), white, NT, preferred_element_type=f32
    )
    scores = both[: n_docs * n_dp] + both[n_docs * n_dp :]
    routed = []
    for o in range(n_dp):
        row = jnp.zeros((n_dp, n_dev * count), f32)
        for d in range(n_docs):
            mine = owners[d] == float(o)
            row += jnp.where(mine, scores[d * n_dp : (d + 1) * n_dp], 0.0)
        routed.append(row)
    scores = jnp.swapaxes(jnp.stack(routed), 0, 1).reshape(n_dp * n_dp, n_dev * count)
    tall = n_hi * n_dp
    for s in range(n_seq):
        lanes = slice(s * n_out, (s + 1) * n_out)
        packed = jnp.concatenate(
            [scores[lo * tall : (lo + 1) * tall, lanes] for lo in range(n_lo)], axis=1
        )
        for hi in range(n_hi):
            out_ref[:, s, hi, :] = packed[hi * n_dp : (hi + 1) * n_dp]


def finish_kernel(parts_ref, out_ref):
    n_hi = parts_ref.shape[1]
    n_dp, n_out = out_ref.shape
    total = jnp.sum(parts_ref[...], axis=0)
    for lo in range(n_dp // n_hi):
        out_ref[lo * n_hi : (lo + 1) * n_hi, :] = total[:, lo * n_out : (lo + 1) * n_out]


def by_features(
    activations,
    out_grads,
    proj_in,
    proj_out,
    queries,
    basis_a,
    basis_g,
    eigen,
    spans,
    doc_owner,
    doc_lengths,
):
    n_dp, n_seq = lax.axis_size("dp"), lax.axis_size("seq")
    n_dev = n_dp * n_seq
    wa, wg = eigen.shape
    count = queries.shape[0]
    share = wa // n_dev
    n_docs = doc_owner.shape[1]
    height = share * (n_docs + count + 1)
    n_out = n_dev * count // n_seq
    n_hi = n_dp * n_out // 128
    bf16, f32 = jnp.bfloat16, jnp.float32
    steps = 5
    part = activations.shape[1] // steps
    vmem = pl.BlockSpec(memory_space=pltpu.VMEM)
    hbm = pl.BlockSpec(memory_space=pltpu.HBM)
    small = (queries, basis_a, basis_g, eigen)
    integers = (spans, doc_owner, doc_lengths)
    large = (activations, out_grads, proj_in, proj_out)
    operands = small + integers + large
    copied = (
        [pltpu.VMEM(x.shape, x.dtype) for x in small]
        + [pltpu.SMEM(x.shape, x.dtype) for x in integers]
        + [pltpu.VMEM((steps, x.shape[0], part), x.dtype) for x in large]
    )
    blocks = pl.pallas_call(
        functools.partial(features_kernel, steps),
        out_shape=jax.ShapeDtypeStruct((n_dev, height // share, share, wg), bf16),
        in_specs=[hbm] * 11,
        out_specs=vmem,
        scratch_shapes=copied
        + [
            pltpu.VMEM((wa * count, wg), f32),
            pltpu.VMEM((activations.shape[0], wa), f32),
            pltpu.VMEM((activations.shape[0], wg), f32),
            pltpu.VMEM((height, n_dev, wg), f32),
            pltpu.SemaphoreType.DMA((7,)),
            pltpu.SemaphoreType.DMA((steps, 4)),
        ],
        compiler_params=pltpu.CompilerParams(vmem_limit_bytes=features_bytes),
        name="features",
    )(*(pltpu.with_memory_space_constraint(x, pltpu.HBM) for x in operands))
    everywhere = functools.partial(
        lax.all_to_all,
        axis_name=("dp", "seq"),
        split_axis=0,
        concat_axis=0,
        tiled=True,
    )
    blocks = everywhere(blocks)
    parts = pl.pallas_call(
        functools.partial(partial_kernel, n_docs),
        out_shape=jax.ShapeDtypeStruct((n_dp, n_seq, n_hi, 128), f32),
        in_specs=[vmem],
        out_specs=vmem,
        scratch_shapes=[
            pltpu.VMEM((n_dev, share, wg), f32),
            pltpu.VMEM((share, n_dev * count, wg), f32),
        ],
        compiler_params=pltpu.CompilerParams(vmem_limit_bytes=small_bytes),
        name="partial",
    )(blocks)
    parts = everywhere(parts.reshape(n_dev, n_hi, 128))
    result = pl.pallas_call(
        finish_kernel,
        out_shape=jax.ShapeDtypeStruct((n_dp, n_out), f32),
        in_specs=[vmem],
        out_specs=vmem,
        compiler_params=pltpu.CompilerParams(vmem_limit_bytes=small_bytes),
        name="finish",
    )(parts)
    return result[None]


def by_rows(
    activations,
    out_grads,
    proj_in,
    proj_out,
    queries,
    basis_a,
    basis_g,
    eigen,
    spans,
    doc_owner,
    doc_lengths,
):
    n_dp, n_seq = lax.axis_size("dp"), lax.axis_size("seq")
    n_dev = n_dp * n_seq
    rows, width = activations.shape
    wa, wg = eigen.shape
    count = queries.shape[0]
    share = wa // n_seq
    steps = 5
    part = width // steps
    bf16, f32 = jnp.bfloat16, jnp.float32
    params = pltpu.CompilerParams(vmem_limit_bytes=vmem_bytes)
    vmem = pl.BlockSpec(memory_space=pltpu.VMEM)
    hbm = pl.BlockSpec(memory_space=pltpu.HBM)

    outgoing = pl.pallas_call(
        whiten_kernel,
        out_shape=jax.ShapeDtypeStruct((n_dp, n_seq, count, share, wg), bf16),
        in_specs=[vmem] * 4,
        out_specs=vmem,
        scratch_shapes=[pltpu.VMEM((wa * count, wg), f32)],
        compiler_params=params,
        name="whiten",
    )(queries, basis_a, basis_g, eigen)
    white = lax.all_to_all(
        outgoing.reshape(n_dev, count, share, wg),
        ("dp", "seq"),
        split_axis=0,
        concat_axis=0,
        tiled=True,
    )

    docs = pl.pallas_call(
        functools.partial(docs_kernel, steps),
        out_shape=jax.ShapeDtypeStruct((n_dp, n_seq, share, wg), bf16),
        in_specs=[hbm] * 8,
        out_specs=vmem,
        scratch_shapes=[
            pltpu.VMEM((steps, rows, part), bf16),
            pltpu.VMEM((steps, rows, part), bf16),
            pltpu.VMEM((steps, wa, part), bf16),
            pltpu.VMEM((steps, wg, part), bf16),
            pltpu.SMEM(spans.shape, jnp.int32),
            pltpu.SMEM(doc_owner.shape, jnp.int32),
            pltpu.SMEM(doc_lengths.shape, jnp.int32),
            pltpu.SemaphoreType.DMA((steps, 4)),
            pltpu.SemaphoreType.DMA((3,)),
        ],
        compiler_params=params,
        name="docs",
    )(
        spans,
        doc_owner,
        doc_lengths,
        activations,
        out_grads,
        proj_in,
        proj_out,
        outgoing,
    )
    docs = lax.all_to_all(
        docs.reshape(n_dev, share, wg),
        ("dp", "seq"),
        split_axis=0,
        concat_axis=0,
        tiled=True,
    )

    n_query = n_dev * count
    n_out = n_query // n_seq
    parts = pl.pallas_call(
        score_kernel,
        out_shape=[jax.ShapeDtypeStruct((n_dp, n_out), f32)] * n_seq,
        in_specs=[vmem] * 2,
        out_specs=[vmem] * n_seq,
        scratch_shapes=[pltpu.VMEM((n_query, n_dp * share), f32)],
        compiler_params=params,
        name="score",
    )(docs.reshape(n_dp, n_seq, share, wg), white.reshape(n_query, share, wg))
    result = parts[0]
    for k in range(n_seq - 1, 0, -1):
        pairs = [(i, i ^ k) for i in range(n_seq)]
        result = result + lax.ppermute(parts[k], "seq", pairs)
    return result[None]


def per_device(*args):
    n_dp, n_seq = lax.axis_size("dp"), lax.axis_size("seq")
    n_dev = n_dp * n_seq
    wa, wg = args[7].shape
    count = args[4].shape[0]
    share = wa // n_dev
    n_out = n_dp * count
    fits = (
        share > 0
        and share * n_dev == wa
        and wg == 128
        and n_dp % 8 == 0
        and n_dp <= 256
        and args[9].shape[1] % share == 0
        and 128 % n_out == 0
        and n_dp * n_out % 128 == 0
    )
    return (by_features if fits else by_rows)(*args)


def solution(mesh):
    return jax.shard_map(
        per_device,
        mesh=mesh,
        in_specs=(
            P(("dp", "seq"), None),
            P(("dp", "seq"), None),
            P(),
            P(),
            P(("dp", "seq"), None),
            P(),
            P(),
            P(),
            P("dp", None, None),
            P("dp", None),
            P("dp", None),
        ),
        out_specs=P("dp", None, "seq"),
        check_vma=False,
    )
```

```python
import functools

import jax
import jax.numpy as jnp
from jax import lax
from jax.experimental import pallas as pl
from jax.experimental.pallas import tpu as pltpu
from jax.sharding import PartitionSpec as P

damping = 0.1
vmem_bytes = 64 * 1024 * 1024
features_bytes = 32 * 1024 * 1024
small_bytes = 16 * 1024 * 1024

NT = (((1,), (1,)), ((), ()))
NN = (((1,), (0,)), ((), ()))
TN = (((0,), (0,)), ((), ()))


def whiten_kernel(q_ref, ba_ref, bg_ref, eig_ref, out_ref, rows_ref):
    count = q_ref.shape[0]
    wa, wg = eig_ref.shape
    n_seq = out_ref.shape[1]
    share = wa // n_seq
    dot = functools.partial(
        lax.dot_general,
        precision=lax.Precision.HIGHEST,
        preferred_element_type=jnp.float32,
    )
    for a in range(wa):
        rows_ref[a * count : (a + 1) * count, :] = q_ref[:, a * wg : (a + 1) * wg]
    grid = jnp.concatenate(
        [rows_ref[pl.ds(n, wa, stride=count), :] for n in range(count)], axis=0
    )
    ba, bg = ba_ref[...], bg_ref[...]
    scale = eig_ref[...] + damping
    half = dot(grid, bg, NN)
    back = []
    for n in range(count):
        rotated = dot(ba, half[n * wa : (n + 1) * wa], TN)
        back.append(dot(ba, rotated / scale, NN))
    white = dot(jnp.concatenate(back, axis=0), bg, NT).astype(jnp.bfloat16)
    for n in range(count):
        for s in range(n_seq):
            lo = n * wa + s * share
            block = white[lo : lo + share]
            for o in range(out_ref.shape[0]):
                out_ref[o, s, n] = block


def docs_kernel(
    steps,
    span_hbm,
    owner_hbm,
    length_hbm,
    act_hbm,
    grad_hbm,
    pin_hbm,
    pout_hbm,
    after_hbm,
    out_ref,
    act,
    grad,
    pin,
    pout,
    span_ref,
    owner_ref,
    length_ref,
    sems,
    small_sems,
):
    rows, width = act_hbm.shape
    part = width // steps
    wa = pin_hbm.shape[0]
    n_docs = owner_ref.shape[1]
    n_seq, share, wg = out_ref.shape[1:]
    copies = []
    for k in range(steps):
        cols = pl.ds(k * part, part)
        step = []
        for i, (src, dst) in enumerate(
            ((pin_hbm, pin), (act_hbm, act), (pout_hbm, pout), (grad_hbm, grad))
        ):
            copy = pltpu.make_async_copy(src.at[:, cols], dst.at[k], sems.at[k, i])
            copy.start()
            step.append(copy)
        copies.append(step)
    small = []
    for i, (src, dst) in enumerate(
        ((span_hbm, span_ref), (owner_hbm, owner_ref), (length_hbm, length_ref))
    ):
        copy = pltpu.make_async_copy(src, dst, small_sems.at[i])
        copy.start()
        small.append(copy)
    a_sum = jnp.zeros((rows, wa), jnp.float32)
    g_sum = jnp.zeros((rows, wg), jnp.float32)
    for k in range(steps):
        copies[k][0].wait()
        copies[k][1].wait()
        a_sum += lax.dot_general(
            act[k], pin[k], NT, preferred_element_type=jnp.float32
        )
        copies[k][2].wait()
        copies[k][3].wait()
        g_sum += lax.dot_general(
            grad[k], pout[k], NT, preferred_element_type=jnp.float32
        )
    for copy in small:
        copy.wait()
    a_t = a_sum.T.astype(jnp.bfloat16).astype(jnp.float32)
    g_part = g_sum.astype(jnp.bfloat16)
    me = lax.axis_index("seq")
    position = lax.broadcasted_iota(jnp.int32, (wa, rows), 1)
    start = jnp.int32(0)
    spread = []
    for d in range(n_docs):
        end = start + span_ref[0, me, d]
        inside = (position >= start) & (position < end)
        spread.append(jnp.where(inside, a_t, 0.0).astype(jnp.bfloat16))
        start = end
    sums = jnp.dot(
        jnp.concatenate(spread, axis=0), g_part, preferred_element_type=jnp.float32
    )
    out_ref[...] = jnp.zeros_like(out_ref)
    for d in range(n_docs):
        length = jnp.full((wa, wg), length_ref[0, d], jnp.int32).astype(jnp.float32)
        doc = (sums[d * wa : (d + 1) * wa] / length).astype(jnp.bfloat16)
        out_ref[owner_ref[0, d]] = doc.reshape(n_seq, share, wg)


def score_kernel(docs_ref, white_ref, *refs):
    out_refs, sum_ref = refs[:-1], refs[-1]
    n_dp, n_seq, share, wg = docs_ref.shape
    count = white_ref.shape[0]
    n_out = out_refs[0].shape[1]
    width = n_dp * share
    total = docs_ref[:, 0].astype(jnp.float32)
    for s in range(1, n_seq):
        total += docs_ref[:, s].astype(jnp.float32)
    docs = total.reshape(width, wg).astype(jnp.bfloat16)
    white = white_ref[...].reshape(count * share, wg)
    cross = lax.dot_general(white, docs, NT, preferred_element_type=jnp.float32)
    cross = cross.reshape(count, share, width)
    row = lax.broadcasted_iota(jnp.int32, (share, width), 0)
    col = lax.broadcasted_iota(jnp.int32, (share, width), 1)
    same = (row == col % share)[None]
    sum_ref[...] = jnp.sum(jnp.where(same, cross, 0.0), axis=1)
    owner = lax.broadcasted_iota(jnp.int32, (n_dp, width), 0)
    lane = lax.broadcasted_iota(jnp.int32, (n_dp, width), 1)
    gather = (lane // share == owner).astype(jnp.float32)
    me = lax.axis_index("seq")
    for k in range(n_seq):
        block = sum_ref[pl.ds((me ^ k) * n_out, n_out), :]
        out_refs[k][...] = lax.dot_general(
            gather,
            block,
            NT,
            precision=lax.Precision.HIGHEST,
            preferred_element_type=jnp.float32,
        )


def split_dot(x, w):
    bf16 = jnp.bfloat16
    x_hi, w_hi = x.astype(bf16), w.astype(bf16)
    x_lo = (x - x_hi.astype(jnp.float32)).astype(bf16)
    w_lo = (w - w_hi.astype(jnp.float32)).astype(bf16)
    return jnp.dot(
        jnp.concatenate([x_hi, x_lo, x_hi], axis=1),
        jnp.concatenate([w_hi, w_hi, w_lo], axis=0),
        preferred_element_type=jnp.float32,
    )


def side_by_side(x, count):
    rows = x.shape[0] // count
    return jnp.concatenate(
        [x[n * rows : (n + 1) * rows] for n in range(count)], axis=1
    )


def features_kernel(steps, *refs):
    hbm_refs, out_ref, local_refs = refs[:11], refs[11], refs[12:23]
    rows_ref, a_sum, g_sum, blocks, small_sems, sems = refs[23:]
    q, ba_ref, bg_ref, eig_ref, span, owner, length, act, grad, pin, pout = local_refs
    bf16, f32 = jnp.bfloat16, jnp.float32
    count = q.shape[0]
    wa, wg = eig_ref.shape
    rows, part = act.shape[1:]
    n_docs = owner.shape[1]
    n_dev = out_ref.shape[0]
    share = wa // n_dev
    dot = functools.partial(lax.dot_general, preferred_element_type=f32)

    def chunk(k):
        cols = pl.ds(pl.multiple_of(k * part, part), part)
        return [
            pltpu.make_async_copy(
                hbm_refs[7 + i].at[:, cols], local_refs[7 + i].at[k], sems.at[k, i]
            )
            for i in (2, 0, 3, 1)
        ]

    small = []
    for i in range(7):
        copy = pltpu.make_async_copy(hbm_refs[i], local_refs[i], small_sems.at[i])
        copy.start()
        small.append(copy)
    for k in range(steps):
        for copy in chunk(k):
            copy.start(priority=1)
    a_sum[...] = jnp.zeros_like(a_sum)
    g_sum[...] = jnp.zeros_like(g_sum)

    def write_tiles(first, tiles):
        table = jnp.swapaxes(blocks[: tiles * share], 0, 1)
        for i in range(tiles):
            tile = table[:, i * share : (i + 1) * share]
            out_ref[:, first + i] = tile.astype(bf16)

    def whiten():
        for copy in small[:4]:
            copy.wait()
        for a in range(wa):
            rows_ref[a * count : (a + 1) * count, :] = q[:, a * wg : (a + 1) * wg]
        grid = jnp.concatenate(
            [rows_ref[pl.ds(n, wa, stride=count), :] for n in range(count)], axis=0
        )
        ba, bg = ba_ref[...], bg_ref[...]
        scale = jnp.concatenate([eig_ref[...] + damping] * count, axis=1)
        rotated = split_dot(ba.T, side_by_side(split_dot(grid, bg), count))
        back = split_dot(ba, rotated / scale)
        back = jnp.concatenate(
            [back[:, n * wg : (n + 1) * wg] for n in range(count)], axis=0
        )
        white = split_dot(back, bg.T)
        for r in range(share):
            for n in range(count):
                lo = n * wa + r * n_dev
                blocks[n * share + r] = white[lo : lo + n_dev]
        write_tiles(n_docs, count)

    def add_chunk(k, carry):
        for copy in chunk(k):
            copy.wait()
        a_sum[...] += dot(act[k], pin[k], NT)
        g_sum[...] += dot(grad[k], pout[k], NT)
        return carry

    whiten()
    for copy in small[4:]:
        copy.wait()
    row = lax.broadcasted_iota(jnp.int32, (share, wg), 0)
    lane = lax.broadcasted_iota(jnp.int32, (share, wg), 1)
    each = n_docs // share
    place = row * each + lax.div(lane, wg // each)
    target = jnp.full((share, wg), owner[0, 0], jnp.int32)
    for d in range(1, n_docs):
        target = jnp.where(place == d, owner[0, d], target)
    target = jnp.broadcast_to(target.astype(f32)[None], (n_dev, share, wg))
    out_ref[:, n_docs + count] = target.astype(bf16)
    lax.fori_loop(0, steps, add_chunk, 0)
    a_part = a_sum[...].T.astype(bf16).astype(f32)
    g_part = g_sum[...].astype(bf16)
    me = lax.axis_index("seq")
    position = lax.broadcasted_iota(jnp.int32, (wa, rows), 1)
    start = jnp.int32(0)
    spread = []
    for d in range(n_docs):
        end = start + span[0, me, d]
        inside = (position >= start) & (position < end)
        spread.append(jnp.where(inside, a_part, 0.0).astype(bf16))
        start = end
    sums = dot(jnp.concatenate(spread, axis=0), g_part, NN)
    for d in range(n_docs):
        tokens = jnp.full((n_dev, wg), length[0, d], jnp.int32).astype(f32)
        for r in range(share):
            lo = d * wa + r * n_dev
            blocks[d * share + r] = sums[lo : lo + n_dev] / tokens
    write_tiles(0, n_docs)


def partial_kernel(n_docs, block_ref, out_ref, rows_ref, white_ref):
    bf16, f32 = jnp.bfloat16, jnp.float32
    n_dp, n_seq, n_hi = out_ref.shape[:3]
    n_dev, slots, share, wg = block_ref.shape
    count = slots - n_docs - 1
    n_out = n_dev * count // n_seq
    n_lo = n_dp // n_hi
    for d in range(n_docs):
        part = block_ref[:, d].astype(f32).reshape(n_dp, n_seq, share, wg)
        total = part[:, 0]
        for s in range(1, n_seq):
            total += part[:, s]
        rows_ref[d, :n_dp] = total
    for n in range(n_docs, n_docs + count):
        rows_ref[n] = block_ref[:, n].astype(f32)
    part = block_ref[:, n_docs + count].astype(f32)
    rows_ref[n_docs + count, :n_dp] = part.reshape(n_dp, n_seq, share, wg)[:, 0]
    for n in range(count):
        for r in range(share):
            white_ref[r, pl.ds(n, n_dev, stride=count), :] = rows_ref[n_docs + n, :, r]
    docs = jnp.concatenate(
        [
            jnp.concatenate([rows_ref[d, :n_dp, r] for d in range(n_docs)], axis=0)
            for r in range(share)
        ],
        axis=1,
    )
    white = jnp.concatenate([white_ref[r] for r in range(share)], axis=1).astype(bf16)
    each = n_docs // share
    owners = []
    for d in range(n_docs):
        lane = d % each * (wg // each)
        column = rows_ref[n_docs + count, :n_dp, d // each][:, lane : lane + 1]
        owners.append(jnp.broadcast_to(column, (n_dp, n_dev * count)))
    upper = docs.astype(bf16)
    lower = (docs - upper.astype(f32)).astype(bf16)
    both = lax.dot_general(
        jnp.concatenate([upper, lower], axis=0), white, NT, preferred_element_type=f32
    )
    scores = both[: n_docs * n_dp] + both[n_docs * n_dp :]
    routed = []
    for o in range(n_dp):
        row = jnp.zeros((n_dp, n_dev * count), f32)
        for d in range(n_docs):
            mine = owners[d] == float(o)
            row += jnp.where(mine, scores[d * n_dp : (d + 1) * n_dp], 0.0)
        routed.append(row)
    scores = jnp.swapaxes(jnp.stack(routed), 0, 1).reshape(n_dp * n_dp, n_dev * count)
    tall = n_hi * n_dp
    for s in range(n_seq):
        lanes = slice(s * n_out, (s + 1) * n_out)
        packed = jnp.concatenate(
            [scores[lo * tall : (lo + 1) * tall, lanes] for lo in range(n_lo)], axis=1
        )
        for hi in range(n_hi):
            out_ref[:, s, hi, :] = packed[hi * n_dp : (hi + 1) * n_dp]


def finish_kernel(parts_ref, out_ref):
    n_hi = parts_ref.shape[1]
    n_dp, n_out = out_ref.shape
    total = jnp.sum(parts_ref[...], axis=0)
    for lo in range(n_dp // n_hi):
        out_ref[lo * n_hi : (lo + 1) * n_hi, :] = total[:, lo * n_out : (lo + 1) * n_out]


def by_features(
    activations,
    out_grads,
    proj_in,
    proj_out,
    queries,
    basis_a,
    basis_g,
    eigen,
    spans,
    doc_owner,
    doc_lengths,
):
    n_dp, n_seq = lax.axis_size("dp"), lax.axis_size("seq")
    n_dev = n_dp * n_seq
    wa, wg = eigen.shape
    count = queries.shape[0]
    share = wa // n_dev
    n_docs = doc_owner.shape[1]
    height = share * (n_docs + count + 1)
    n_out = n_dev * count // n_seq
    n_hi = n_dp * n_out // 128
    bf16, f32 = jnp.bfloat16, jnp.float32
    steps = 5
    part = activations.shape[1] // steps
    vmem = pl.BlockSpec(memory_space=pltpu.VMEM)
    hbm = pl.BlockSpec(memory_space=pltpu.HBM)
    small = (queries, basis_a, basis_g, eigen)
    integers = (spans, doc_owner, doc_lengths)
    large = (activations, out_grads, proj_in, proj_out)
    operands = small + integers + large
    copied = (
        [pltpu.VMEM(x.shape, x.dtype) for x in small]
        + [pltpu.SMEM(x.shape, x.dtype) for x in integers]
        + [pltpu.VMEM((steps, x.shape[0], part), x.dtype) for x in large]
    )
    blocks = pl.pallas_call(
        functools.partial(features_kernel, steps),
        out_shape=jax.ShapeDtypeStruct((n_dev, height // share, share, wg), bf16),
        in_specs=[hbm] * 11,
        out_specs=vmem,
        scratch_shapes=copied
        + [
            pltpu.VMEM((wa * count, wg), f32),
            pltpu.VMEM((activations.shape[0], wa), f32),
            pltpu.VMEM((activations.shape[0], wg), f32),
            pltpu.VMEM((share * max(n_docs, count), n_dev, wg), f32),
            pltpu.SemaphoreType.DMA((7,)),
            pltpu.SemaphoreType.DMA((steps, 4)),
        ],
        compiler_params=pltpu.CompilerParams(vmem_limit_bytes=features_bytes),
        name="features",
    )(*(pltpu.with_memory_space_constraint(x, pltpu.HBM) for x in operands))
    everywhere = functools.partial(
        lax.all_to_all,
        axis_name=("dp", "seq"),
        split_axis=0,
        concat_axis=0,
        tiled=True,
    )
    blocks = everywhere(blocks)
    parts = pl.pallas_call(
        functools.partial(partial_kernel, n_docs),
        out_shape=jax.ShapeDtypeStruct((n_dp, n_seq, n_hi, 128), f32),
        in_specs=[vmem],
        out_specs=vmem,
        scratch_shapes=[
            pltpu.VMEM((height // share, n_dev, share, wg), f32),
            pltpu.VMEM((share, n_dev * count, wg), f32),
        ],
        compiler_params=pltpu.CompilerParams(vmem_limit_bytes=small_bytes),
        name="partial",
    )(blocks)
    parts = everywhere(parts.reshape(n_dev, n_hi, 128))
    result = pl.pallas_call(
        finish_kernel,
        out_shape=jax.ShapeDtypeStruct((n_dp, n_out), f32),
        in_specs=[vmem],
        out_specs=vmem,
        compiler_params=pltpu.CompilerParams(vmem_limit_bytes=small_bytes),
        name="finish",
    )(parts)
    return result[None]


def by_rows(
    activations,
    out_grads,
    proj_in,
    proj_out,
    queries,
    basis_a,
    basis_g,
    eigen,
    spans,
    doc_owner,
    doc_lengths,
):
    n_dp, n_seq = lax.axis_size("dp"), lax.axis_size("seq")
    n_dev = n_dp * n_seq
    rows, width = activations.shape
    wa, wg = eigen.shape
    count = queries.shape[0]
    share = wa // n_seq
    steps = 5
    part = width // steps
    bf16, f32 = jnp.bfloat16, jnp.float32
    params = pltpu.CompilerParams(vmem_limit_bytes=vmem_bytes)
    vmem = pl.BlockSpec(memory_space=pltpu.VMEM)
    hbm = pl.BlockSpec(memory_space=pltpu.HBM)

    outgoing = pl.pallas_call(
        whiten_kernel,
        out_shape=jax.ShapeDtypeStruct((n_dp, n_seq, count, share, wg), bf16),
        in_specs=[vmem] * 4,
        out_specs=vmem,
        scratch_shapes=[pltpu.VMEM((wa * count, wg), f32)],
        compiler_params=params,
        name="whiten",
    )(queries, basis_a, basis_g, eigen)
    white = lax.all_to_all(
        outgoing.reshape(n_dev, count, share, wg),
        ("dp", "seq"),
        split_axis=0,
        concat_axis=0,
        tiled=True,
    )

    docs = pl.pallas_call(
        functools.partial(docs_kernel, steps),
        out_shape=jax.ShapeDtypeStruct((n_dp, n_seq, share, wg), bf16),
        in_specs=[hbm] * 8,
        out_specs=vmem,
        scratch_shapes=[
            pltpu.VMEM((steps, rows, part), bf16),
            pltpu.VMEM((steps, rows, part), bf16),
            pltpu.VMEM((steps, wa, part), bf16),
            pltpu.VMEM((steps, wg, part), bf16),
            pltpu.SMEM(spans.shape, jnp.int32),
            pltpu.SMEM(doc_owner.shape, jnp.int32),
            pltpu.SMEM(doc_lengths.shape, jnp.int32),
            pltpu.SemaphoreType.DMA((steps, 4)),
            pltpu.SemaphoreType.DMA((3,)),
        ],
        compiler_params=params,
        name="docs",
    )(
        spans,
        doc_owner,
        doc_lengths,
        activations,
        out_grads,
        proj_in,
        proj_out,
        outgoing,
    )
    docs = lax.all_to_all(
        docs.reshape(n_dev, share, wg),
        ("dp", "seq"),
        split_axis=0,
        concat_axis=0,
        tiled=True,
    )

    n_query = n_dev * count
    n_out = n_query // n_seq
    parts = pl.pallas_call(
        score_kernel,
        out_shape=[jax.ShapeDtypeStruct((n_dp, n_out), f32)] * n_seq,
        in_specs=[vmem] * 2,
        out_specs=[vmem] * n_seq,
        scratch_shapes=[pltpu.VMEM((n_query, n_dp * share), f32)],
        compiler_params=params,
        name="score",
    )(docs.reshape(n_dp, n_seq, share, wg), white.reshape(n_query, share, wg))
    result = parts[0]
    for k in range(n_seq - 1, 0, -1):
        pairs = [(i, i ^ k) for i in range(n_seq)]
        result = result + lax.ppermute(parts[k], "seq", pairs)
    return result[None]


def per_device(*args):
    n_dp, n_seq = lax.axis_size("dp"), lax.axis_size("seq")
    n_dev = n_dp * n_seq
    wa, wg = args[7].shape
    count = args[4].shape[0]
    share = wa // n_dev
    n_out = n_dp * count
    fits = (
        share > 0
        and share * n_dev == wa
        and wg == 128
        and n_dp % 8 == 0
        and n_dp <= 256
        and args[9].shape[1] % share == 0
        and 128 % n_out == 0
        and n_dp * n_out % 128 == 0
    )
    return (by_features if fits else by_rows)(*args)


def solution(mesh):
    return jax.shard_map(
        per_device,
        mesh=mesh,
        in_specs=(
            P(("dp", "seq"), None),
            P(("dp", "seq"), None),
            P(),
            P(),
            P(("dp", "seq"), None),
            P(),
            P(),
            P(),
            P("dp", None, None),
            P("dp", None),
            P("dp", None),
        ),
        out_specs=P("dp", None, "seq"),
        check_vma=False,
    )
```

```python
import functools

import jax
import jax.numpy as jnp
from jax import lax
from jax.experimental import pallas as pl
from jax.experimental.pallas import tpu as pltpu
from jax.sharding import PartitionSpec as P

damping = 0.1
vmem_bytes = 64 * 1024 * 1024
features_bytes = 32 * 1024 * 1024
small_bytes = 16 * 1024 * 1024

NT = (((1,), (1,)), ((), ()))
NN = (((1,), (0,)), ((), ()))
TN = (((0,), (0,)), ((), ()))


def whiten_kernel(q_ref, ba_ref, bg_ref, eig_ref, out_ref, rows_ref):
    count = q_ref.shape[0]
    wa, wg = eig_ref.shape
    n_seq = out_ref.shape[1]
    share = wa // n_seq
    dot = functools.partial(
        lax.dot_general,
        precision=lax.Precision.HIGHEST,
        preferred_element_type=jnp.float32,
    )
    for a in range(wa):
        rows_ref[a * count : (a + 1) * count, :] = q_ref[:, a * wg : (a + 1) * wg]
    grid = jnp.concatenate(
        [rows_ref[pl.ds(n, wa, stride=count), :] for n in range(count)], axis=0
    )
    ba, bg = ba_ref[...], bg_ref[...]
    scale = eig_ref[...] + damping
    half = dot(grid, bg, NN)
    back = []
    for n in range(count):
        rotated = dot(ba, half[n * wa : (n + 1) * wa], TN)
        back.append(dot(ba, rotated / scale, NN))
    white = dot(jnp.concatenate(back, axis=0), bg, NT).astype(jnp.bfloat16)
    for n in range(count):
        for s in range(n_seq):
            lo = n * wa + s * share
            block = white[lo : lo + share]
            for o in range(out_ref.shape[0]):
                out_ref[o, s, n] = block


def docs_kernel(
    steps,
    span_hbm,
    owner_hbm,
    length_hbm,
    act_hbm,
    grad_hbm,
    pin_hbm,
    pout_hbm,
    after_hbm,
    out_ref,
    act,
    grad,
    pin,
    pout,
    span_ref,
    owner_ref,
    length_ref,
    sems,
    small_sems,
):
    rows, width = act_hbm.shape
    part = width // steps
    wa = pin_hbm.shape[0]
    n_docs = owner_ref.shape[1]
    n_seq, share, wg = out_ref.shape[1:]
    copies = []
    for k in range(steps):
        cols = pl.ds(k * part, part)
        step = []
        for i, (src, dst) in enumerate(
            ((pin_hbm, pin), (act_hbm, act), (pout_hbm, pout), (grad_hbm, grad))
        ):
            copy = pltpu.make_async_copy(src.at[:, cols], dst.at[k], sems.at[k, i])
            copy.start()
            step.append(copy)
        copies.append(step)
    small = []
    for i, (src, dst) in enumerate(
        ((span_hbm, span_ref), (owner_hbm, owner_ref), (length_hbm, length_ref))
    ):
        copy = pltpu.make_async_copy(src, dst, small_sems.at[i])
        copy.start()
        small.append(copy)
    a_sum = jnp.zeros((rows, wa), jnp.float32)
    g_sum = jnp.zeros((rows, wg), jnp.float32)
    for k in range(steps):
        copies[k][0].wait()
        copies[k][1].wait()
        a_sum += lax.dot_general(
            act[k], pin[k], NT, preferred_element_type=jnp.float32
        )
        copies[k][2].wait()
        copies[k][3].wait()
        g_sum += lax.dot_general(
            grad[k], pout[k], NT, preferred_element_type=jnp.float32
        )
    for copy in small:
        copy.wait()
    a_t = a_sum.T.astype(jnp.bfloat16).astype(jnp.float32)
    g_part = g_sum.astype(jnp.bfloat16)
    me = lax.axis_index("seq")
    position = lax.broadcasted_iota(jnp.int32, (wa, rows), 1)
    start = jnp.int32(0)
    spread = []
    for d in range(n_docs):
        end = start + span_ref[0, me, d]
        inside = (position >= start) & (position < end)
        spread.append(jnp.where(inside, a_t, 0.0).astype(jnp.bfloat16))
        start = end
    sums = jnp.dot(
        jnp.concatenate(spread, axis=0), g_part, preferred_element_type=jnp.float32
    )
    out_ref[...] = jnp.zeros_like(out_ref)
    for d in range(n_docs):
        length = jnp.full((wa, wg), length_ref[0, d], jnp.int32).astype(jnp.float32)
        doc = (sums[d * wa : (d + 1) * wa] / length).astype(jnp.bfloat16)
        out_ref[owner_ref[0, d]] = doc.reshape(n_seq, share, wg)


def score_kernel(docs_ref, white_ref, *refs):
    out_refs, sum_ref = refs[:-1], refs[-1]
    n_dp, n_seq, share, wg = docs_ref.shape
    count = white_ref.shape[0]
    n_out = out_refs[0].shape[1]
    width = n_dp * share
    total = docs_ref[:, 0].astype(jnp.float32)
    for s in range(1, n_seq):
        total += docs_ref[:, s].astype(jnp.float32)
    docs = total.reshape(width, wg).astype(jnp.bfloat16)
    white = white_ref[...].reshape(count * share, wg)
    cross = lax.dot_general(white, docs, NT, preferred_element_type=jnp.float32)
    cross = cross.reshape(count, share, width)
    row = lax.broadcasted_iota(jnp.int32, (share, width), 0)
    col = lax.broadcasted_iota(jnp.int32, (share, width), 1)
    same = (row == col % share)[None]
    sum_ref[...] = jnp.sum(jnp.where(same, cross, 0.0), axis=1)
    owner = lax.broadcasted_iota(jnp.int32, (n_dp, width), 0)
    lane = lax.broadcasted_iota(jnp.int32, (n_dp, width), 1)
    gather = (lane // share == owner).astype(jnp.float32)
    me = lax.axis_index("seq")
    for k in range(n_seq):
        block = sum_ref[pl.ds((me ^ k) * n_out, n_out), :]
        out_refs[k][...] = lax.dot_general(
            gather,
            block,
            NT,
            precision=lax.Precision.HIGHEST,
            preferred_element_type=jnp.float32,
        )


def split_dot(x, w):
    bf16 = jnp.bfloat16
    x_hi, w_hi = x.astype(bf16), w.astype(bf16)
    x_lo = (x - x_hi.astype(jnp.float32)).astype(bf16)
    w_lo = (w - w_hi.astype(jnp.float32)).astype(bf16)
    return jnp.dot(
        jnp.concatenate([x_hi, x_lo, x_hi], axis=1),
        jnp.concatenate([w_hi, w_hi, w_lo], axis=0),
        preferred_element_type=jnp.float32,
    )


def side_by_side(x, count):
    rows = x.shape[0] // count
    return jnp.concatenate(
        [x[n * rows : (n + 1) * rows] for n in range(count)], axis=1
    )


def features_kernel(steps, *refs):
    hbm_refs, out_ref, local_refs = refs[:11], refs[11], refs[12:23]
    rows_ref, a_sum, g_sum, blocks, small_sems, sems = refs[23:]
    q, ba_ref, bg_ref, eig_ref, span, owner, length, act, grad, pin, pout = local_refs
    bf16, f32 = jnp.bfloat16, jnp.float32
    count = q.shape[0]
    wa, wg = eig_ref.shape
    rows, part = act.shape[1:]
    n_docs = owner.shape[1]
    n_dev = out_ref.shape[0]
    share = wa // n_dev
    dot = functools.partial(lax.dot_general, preferred_element_type=f32)

    def chunk(k):
        cols = pl.ds(pl.multiple_of(k * part, part), part)
        return [
            pltpu.make_async_copy(
                hbm_refs[7 + i].at[:, cols], local_refs[7 + i].at[k], sems.at[k, i]
            )
            for i in range(4)
        ]

    small = []
    for i in range(7):
        copy = pltpu.make_async_copy(hbm_refs[i], local_refs[i], small_sems.at[i])
        copy.start()
        small.append(copy)
    for k in range(steps):
        for copy in chunk(k):
            copy.start(priority=1)
    a_sum[...] = jnp.zeros_like(a_sum)
    g_sum[...] = jnp.zeros_like(g_sum)

    def write_tiles(first, tiles):
        table = jnp.swapaxes(blocks[: tiles * share], 0, 1)
        for i in range(tiles):
            tile = table[:, i * share : (i + 1) * share]
            out_ref[:, first + i] = tile.astype(bf16)

    def whiten():
        for copy in small[:4]:
            copy.wait()
        for a in range(wa):
            rows_ref[a * count : (a + 1) * count, :] = q[:, a * wg : (a + 1) * wg]
        grid = jnp.concatenate(
            [rows_ref[pl.ds(n, wa, stride=count), :] for n in range(count)], axis=0
        )
        ba, bg = ba_ref[...], bg_ref[...]
        scale = jnp.concatenate([eig_ref[...] + damping] * count, axis=1)
        rotated = split_dot(ba.T, side_by_side(split_dot(grid, bg), count))
        back = split_dot(ba, rotated / scale)
        back = jnp.concatenate(
            [back[:, n * wg : (n + 1) * wg] for n in range(count)], axis=0
        )
        white = split_dot(back, bg.T)
        for r in range(share):
            for n in range(count):
                lo = n * wa + r * n_dev
                blocks[n * share + r] = white[lo : lo + n_dev]
        write_tiles(n_docs, count)

    def add_chunk(k, carry):
        for copy in chunk(k):
            copy.wait()
        a_sum[...] += dot(act[k], pin[k], NT)
        g_sum[...] += dot(grad[k], pout[k], NT)
        return carry

    whiten()
    for copy in small[4:]:
        copy.wait()
    row = lax.broadcasted_iota(jnp.int32, (share, wg), 0)
    lane = lax.broadcasted_iota(jnp.int32, (share, wg), 1)
    each = n_docs // share
    place = row * each + lax.div(lane, wg // each)
    target = jnp.full((share, wg), owner[0, 0], jnp.int32)
    for d in range(1, n_docs):
        target = jnp.where(place == d, owner[0, d], target)
    target = jnp.broadcast_to(target.astype(f32)[None], (n_dev, share, wg))
    out_ref[:, n_docs + count] = target.astype(bf16)
    lax.fori_loop(0, steps - 1, add_chunk, 0)
    add_chunk(steps - 1, 0)
    a_part = a_sum[...].T.astype(bf16).astype(f32)
    g_part = g_sum[...].astype(bf16)
    me = lax.axis_index("seq")
    position = lax.broadcasted_iota(jnp.int32, (wa, rows), 1)
    start = jnp.int32(0)
    spread = []
    for d in range(n_docs):
        end = start + span[0, me, d]
        inside = (position >= start) & (position < end)
        spread.append(jnp.where(inside, a_part, 0.0).astype(bf16))
        start = end
    sums = dot(jnp.concatenate(spread, axis=0), g_part, NN)
    for d in range(n_docs):
        tokens = jnp.full((n_dev, wg), length[0, d], jnp.int32).astype(f32)
        for r in range(share):
            lo = d * wa + r * n_dev
            blocks[d * share + r] = sums[lo : lo + n_dev] / tokens
    write_tiles(0, n_docs)


def partial_kernel(n_docs, block_ref, out_ref, rows_ref, white_ref):
    bf16, f32 = jnp.bfloat16, jnp.float32
    n_dp, n_seq, n_hi = out_ref.shape[:3]
    n_dev, slots, share, wg = block_ref.shape
    count = slots - n_docs - 1
    n_out = n_dev * count // n_seq
    n_lo = n_dp // n_hi
    for d in range(n_docs):
        part = block_ref[:, d].astype(f32).reshape(n_dp, n_seq, share, wg)
        total = part[:, 0]
        for s in range(1, n_seq):
            total += part[:, s]
        rows_ref[d, :n_dp] = total
    for n in range(n_docs, n_docs + count):
        rows_ref[n] = block_ref[:, n].astype(f32)
    part = block_ref[:, n_docs + count].astype(f32)
    rows_ref[n_docs + count, :n_dp] = part.reshape(n_dp, n_seq, share, wg)[:, 0]
    for n in range(count):
        for r in range(share):
            white_ref[r, pl.ds(n, n_dev, stride=count), :] = rows_ref[n_docs + n, :, r]
    docs = jnp.concatenate(
        [
            jnp.concatenate([rows_ref[d, :n_dp, r] for d in range(n_docs)], axis=0)
            for r in range(share)
        ],
        axis=1,
    )
    white = jnp.concatenate([white_ref[r] for r in range(share)], axis=1).astype(bf16)
    each = n_docs // share
    owners = []
    for d in range(n_docs):
        lane = d % each * (wg // each)
        column = rows_ref[n_docs + count, :n_dp, d // each][:, lane : lane + 1]
        owners.append(jnp.broadcast_to(column, (n_dp, n_dev * count)))
    upper = docs.astype(bf16)
    lower = (docs - upper.astype(f32)).astype(bf16)
    both = lax.dot_general(
        jnp.concatenate([upper, lower], axis=0), white, NT, preferred_element_type=f32
    )
    scores = both[: n_docs * n_dp] + both[n_docs * n_dp :]
    routed = []
    for o in range(n_dp):
        row = jnp.zeros((n_dp, n_dev * count), f32)
        for d in range(n_docs):
            mine = owners[d] == float(o)
            row += jnp.where(mine, scores[d * n_dp : (d + 1) * n_dp], 0.0)
        routed.append(row)
    scores = jnp.swapaxes(jnp.stack(routed), 0, 1).reshape(n_dp * n_dp, n_dev * count)
    tall = n_hi * n_dp
    for s in range(n_seq):
        lanes = slice(s * n_out, (s + 1) * n_out)
        packed = jnp.concatenate(
            [scores[lo * tall : (lo + 1) * tall, lanes] for lo in range(n_lo)], axis=1
        )
        for hi in range(n_hi):
            out_ref[:, s, hi, :] = packed[hi * n_dp : (hi + 1) * n_dp]


def finish_kernel(parts_ref, out_ref):
    n_hi = parts_ref.shape[1]
    n_dp, n_out = out_ref.shape
    total = jnp.sum(parts_ref[...], axis=0)
    for lo in range(n_dp // n_hi):
        out_ref[lo * n_hi : (lo + 1) * n_hi, :] = total[:, lo * n_out : (lo + 1) * n_out]


def by_features(
    activations,
    out_grads,
    proj_in,
    proj_out,
    queries,
    basis_a,
    basis_g,
    eigen,
    spans,
    doc_owner,
    doc_lengths,
):
    n_dp, n_seq = lax.axis_size("dp"), lax.axis_size("seq")
    n_dev = n_dp * n_seq
    wa, wg = eigen.shape
    count = queries.shape[0]
    share = wa // n_dev
    n_docs = doc_owner.shape[1]
    height = share * (n_docs + count + 1)
    n_out = n_dev * count // n_seq
    n_hi = n_dp * n_out // 128
    bf16, f32 = jnp.bfloat16, jnp.float32
    steps = 5
    part = activations.shape[1] // steps
    vmem = pl.BlockSpec(memory_space=pltpu.VMEM)
    hbm = pl.BlockSpec(memory_space=pltpu.HBM)
    small = (queries, basis_a, basis_g, eigen)
    integers = (spans, doc_owner, doc_lengths)
    large = (activations, out_grads, proj_in, proj_out)
    operands = small + integers + large
    copied = (
        [pltpu.VMEM(x.shape, x.dtype) for x in small]
        + [pltpu.SMEM(x.shape, x.dtype) for x in integers]
        + [pltpu.VMEM((steps, x.shape[0], part), x.dtype) for x in large]
    )
    blocks = pl.pallas_call(
        functools.partial(features_kernel, steps),
        out_shape=jax.ShapeDtypeStruct((n_dev, height // share, share, wg), bf16),
        in_specs=[hbm] * 11,
        out_specs=vmem,
        scratch_shapes=copied
        + [
            pltpu.VMEM((wa * count, wg), f32),
            pltpu.VMEM((activations.shape[0], wa), f32),
            pltpu.VMEM((activations.shape[0], wg), f32),
            pltpu.VMEM((share * max(n_docs, count), n_dev, wg), f32),
            pltpu.SemaphoreType.DMA((7,)),
            pltpu.SemaphoreType.DMA((steps, 4)),
        ],
        compiler_params=pltpu.CompilerParams(vmem_limit_bytes=features_bytes),
        name="features",
    )(*(pltpu.with_memory_space_constraint(x, pltpu.HBM) for x in operands))
    everywhere = functools.partial(
        lax.all_to_all,
        axis_name=("dp", "seq"),
        split_axis=0,
        concat_axis=0,
        tiled=True,
    )
    blocks = everywhere(blocks)
    parts = pl.pallas_call(
        functools.partial(partial_kernel, n_docs),
        out_shape=jax.ShapeDtypeStruct((n_dp, n_seq, n_hi, 128), f32),
        in_specs=[vmem],
        out_specs=vmem,
        scratch_shapes=[
            pltpu.VMEM((height // share, n_dev, share, wg), f32),
            pltpu.VMEM((share, n_dev * count, wg), f32),
        ],
        compiler_params=pltpu.CompilerParams(vmem_limit_bytes=small_bytes),
        name="partial",
    )(blocks)
    parts = everywhere(parts.reshape(n_dev, n_hi, 128))
    result = pl.pallas_call(
        finish_kernel,
        out_shape=jax.ShapeDtypeStruct((n_dp, n_out), f32),
        in_specs=[vmem],
        out_specs=vmem,
        compiler_params=pltpu.CompilerParams(vmem_limit_bytes=small_bytes),
        name="finish",
    )(parts)
    return result[None]


def by_rows(
    activations,
    out_grads,
    proj_in,
    proj_out,
    queries,
    basis_a,
    basis_g,
    eigen,
    spans,
    doc_owner,
    doc_lengths,
):
    n_dp, n_seq = lax.axis_size("dp"), lax.axis_size("seq")
    n_dev = n_dp * n_seq
    rows, width = activations.shape
    wa, wg = eigen.shape
    count = queries.shape[0]
    share = wa // n_seq
    steps = 5
    part = width // steps
    bf16, f32 = jnp.bfloat16, jnp.float32
    params = pltpu.CompilerParams(vmem_limit_bytes=vmem_bytes)
    vmem = pl.BlockSpec(memory_space=pltpu.VMEM)
    hbm = pl.BlockSpec(memory_space=pltpu.HBM)

    outgoing = pl.pallas_call(
        whiten_kernel,
        out_shape=jax.ShapeDtypeStruct((n_dp, n_seq, count, share, wg), bf16),
        in_specs=[vmem] * 4,
        out_specs=vmem,
        scratch_shapes=[pltpu.VMEM((wa * count, wg), f32)],
        compiler_params=params,
        name="whiten",
    )(queries, basis_a, basis_g, eigen)
    white = lax.all_to_all(
        outgoing.reshape(n_dev, count, share, wg),
        ("dp", "seq"),
        split_axis=0,
        concat_axis=0,
        tiled=True,
    )

    docs = pl.pallas_call(
        functools.partial(docs_kernel, steps),
        out_shape=jax.ShapeDtypeStruct((n_dp, n_seq, share, wg), bf16),
        in_specs=[hbm] * 8,
        out_specs=vmem,
        scratch_shapes=[
            pltpu.VMEM((steps, rows, part), bf16),
            pltpu.VMEM((steps, rows, part), bf16),
            pltpu.VMEM((steps, wa, part), bf16),
            pltpu.VMEM((steps, wg, part), bf16),
            pltpu.SMEM(spans.shape, jnp.int32),
            pltpu.SMEM(doc_owner.shape, jnp.int32),
            pltpu.SMEM(doc_lengths.shape, jnp.int32),
            pltpu.SemaphoreType.DMA((steps, 4)),
            pltpu.SemaphoreType.DMA((3,)),
        ],
        compiler_params=params,
        name="docs",
    )(
        spans,
        doc_owner,
        doc_lengths,
        activations,
        out_grads,
        proj_in,
        proj_out,
        outgoing,
    )
    docs = lax.all_to_all(
        docs.reshape(n_dev, share, wg),
        ("dp", "seq"),
        split_axis=0,
        concat_axis=0,
        tiled=True,
    )

    n_query = n_dev * count
    n_out = n_query // n_seq
    parts = pl.pallas_call(
        score_kernel,
        out_shape=[jax.ShapeDtypeStruct((n_dp, n_out), f32)] * n_seq,
        in_specs=[vmem] * 2,
        out_specs=[vmem] * n_seq,
        scratch_shapes=[pltpu.VMEM((n_query, n_dp * share), f32)],
        compiler_params=params,
        name="score",
    )(docs.reshape(n_dp, n_seq, share, wg), white.reshape(n_query, share, wg))
    result = parts[0]
    for k in range(n_seq - 1, 0, -1):
        pairs = [(i, i ^ k) for i in range(n_seq)]
        result = result + lax.ppermute(parts[k], "seq", pairs)
    return result[None]


def per_device(*args):
    n_dp, n_seq = lax.axis_size("dp"), lax.axis_size("seq")
    n_dev = n_dp * n_seq
    wa, wg = args[7].shape
    count = args[4].shape[0]
    share = wa // n_dev
    n_out = n_dp * count
    fits = (
        share > 0
        and share * n_dev == wa
        and wg == 128
        and n_dp % 8 == 0
        and n_dp <= 256
        and args[9].shape[1] % share == 0
        and 128 % n_out == 0
        and n_dp * n_out % 128 == 0
    )
    return (by_features if fits else by_rows)(*args)


def solution(mesh):
    return jax.shard_map(
        per_device,
        mesh=mesh,
        in_specs=(
            P(("dp", "seq"), None),
            P(("dp", "seq"), None),
            P(),
            P(),
            P(("dp", "seq"), None),
            P(),
            P(),
            P(),
            P("dp", None, None),
            P("dp", None),
            P("dp", None),
        ),
        out_specs=P("dp", None, "seq"),
        check_vma=False,
    )
```

```python
import functools

import jax
import jax.numpy as jnp
from jax import lax
from jax.experimental import pallas as pl
from jax.experimental.pallas import tpu as pltpu
from jax.sharding import PartitionSpec as P

damping = 0.1
vmem_bytes = 64 * 1024 * 1024
features_bytes = 32 * 1024 * 1024
small_bytes = 16 * 1024 * 1024

NT = (((1,), (1,)), ((), ()))
NN = (((1,), (0,)), ((), ()))
TN = (((0,), (0,)), ((), ()))


def whiten_kernel(q_ref, ba_ref, bg_ref, eig_ref, out_ref, rows_ref):
    count = q_ref.shape[0]
    wa, wg = eig_ref.shape
    n_seq = out_ref.shape[1]
    share = wa // n_seq
    dot = functools.partial(
        lax.dot_general,
        precision=lax.Precision.HIGHEST,
        preferred_element_type=jnp.float32,
    )
    for a in range(wa):
        rows_ref[a * count : (a + 1) * count, :] = q_ref[:, a * wg : (a + 1) * wg]
    grid = jnp.concatenate(
        [rows_ref[pl.ds(n, wa, stride=count), :] for n in range(count)], axis=0
    )
    ba, bg = ba_ref[...], bg_ref[...]
    scale = eig_ref[...] + damping
    half = dot(grid, bg, NN)
    back = []
    for n in range(count):
        rotated = dot(ba, half[n * wa : (n + 1) * wa], TN)
        back.append(dot(ba, rotated / scale, NN))
    white = dot(jnp.concatenate(back, axis=0), bg, NT).astype(jnp.bfloat16)
    for n in range(count):
        for s in range(n_seq):
            lo = n * wa + s * share
            block = white[lo : lo + share]
            for o in range(out_ref.shape[0]):
                out_ref[o, s, n] = block


def docs_kernel(
    steps,
    span_hbm,
    owner_hbm,
    length_hbm,
    act_hbm,
    grad_hbm,
    pin_hbm,
    pout_hbm,
    after_hbm,
    out_ref,
    act,
    grad,
    pin,
    pout,
    span_ref,
    owner_ref,
    length_ref,
    sems,
    small_sems,
):
    rows, width = act_hbm.shape
    part = width // steps
    wa = pin_hbm.shape[0]
    n_docs = owner_ref.shape[1]
    n_seq, share, wg = out_ref.shape[1:]
    copies = []
    for k in range(steps):
        cols = pl.ds(k * part, part)
        step = []
        for i, (src, dst) in enumerate(
            ((pin_hbm, pin), (act_hbm, act), (pout_hbm, pout), (grad_hbm, grad))
        ):
            copy = pltpu.make_async_copy(src.at[:, cols], dst.at[k], sems.at[k, i])
            copy.start()
            step.append(copy)
        copies.append(step)
    small = []
    for i, (src, dst) in enumerate(
        ((span_hbm, span_ref), (owner_hbm, owner_ref), (length_hbm, length_ref))
    ):
        copy = pltpu.make_async_copy(src, dst, small_sems.at[i])
        copy.start()
        small.append(copy)
    a_sum = jnp.zeros((rows, wa), jnp.float32)
    g_sum = jnp.zeros((rows, wg), jnp.float32)
    for k in range(steps):
        copies[k][0].wait()
        copies[k][1].wait()
        a_sum += lax.dot_general(
            act[k], pin[k], NT, preferred_element_type=jnp.float32
        )
        copies[k][2].wait()
        copies[k][3].wait()
        g_sum += lax.dot_general(
            grad[k], pout[k], NT, preferred_element_type=jnp.float32
        )
    for copy in small:
        copy.wait()
    a_t = a_sum.T.astype(jnp.bfloat16).astype(jnp.float32)
    g_part = g_sum.astype(jnp.bfloat16)
    me = lax.axis_index("seq")
    position = lax.broadcasted_iota(jnp.int32, (wa, rows), 1)
    start = jnp.int32(0)
    spread = []
    for d in range(n_docs):
        end = start + span_ref[0, me, d]
        inside = (position >= start) & (position < end)
        spread.append(jnp.where(inside, a_t, 0.0).astype(jnp.bfloat16))
        start = end
    sums = jnp.dot(
        jnp.concatenate(spread, axis=0), g_part, preferred_element_type=jnp.float32
    )
    out_ref[...] = jnp.zeros_like(out_ref)
    for d in range(n_docs):
        length = jnp.full((wa, wg), length_ref[0, d], jnp.int32).astype(jnp.float32)
        doc = (sums[d * wa : (d + 1) * wa] / length).astype(jnp.bfloat16)
        out_ref[owner_ref[0, d]] = doc.reshape(n_seq, share, wg)


def score_kernel(docs_ref, white_ref, *refs):
    out_refs, sum_ref = refs[:-1], refs[-1]
    n_dp, n_seq, share, wg = docs_ref.shape
    count = white_ref.shape[0]
    n_out = out_refs[0].shape[1]
    width = n_dp * share
    total = docs_ref[:, 0].astype(jnp.float32)
    for s in range(1, n_seq):
        total += docs_ref[:, s].astype(jnp.float32)
    docs = total.reshape(width, wg).astype(jnp.bfloat16)
    white = white_ref[...].reshape(count * share, wg)
    cross = lax.dot_general(white, docs, NT, preferred_element_type=jnp.float32)
    cross = cross.reshape(count, share, width)
    row = lax.broadcasted_iota(jnp.int32, (share, width), 0)
    col = lax.broadcasted_iota(jnp.int32, (share, width), 1)
    same = (row == col % share)[None]
    sum_ref[...] = jnp.sum(jnp.where(same, cross, 0.0), axis=1)
    owner = lax.broadcasted_iota(jnp.int32, (n_dp, width), 0)
    lane = lax.broadcasted_iota(jnp.int32, (n_dp, width), 1)
    gather = (lane // share == owner).astype(jnp.float32)
    me = lax.axis_index("seq")
    for k in range(n_seq):
        block = sum_ref[pl.ds((me ^ k) * n_out, n_out), :]
        out_refs[k][...] = lax.dot_general(
            gather,
            block,
            NT,
            precision=lax.Precision.HIGHEST,
            preferred_element_type=jnp.float32,
        )


def split_dot(x, w):
    bf16 = jnp.bfloat16
    x_hi, w_hi = x.astype(bf16), w.astype(bf16)
    x_lo = (x - x_hi.astype(jnp.float32)).astype(bf16)
    w_lo = (w - w_hi.astype(jnp.float32)).astype(bf16)
    return jnp.dot(
        jnp.concatenate([x_hi, x_lo, x_hi], axis=1),
        jnp.concatenate([w_hi, w_hi, w_lo], axis=0),
        preferred_element_type=jnp.float32,
    )


def side_by_side(x, count):
    rows = x.shape[0] // count
    return jnp.concatenate(
        [x[n * rows : (n + 1) * rows] for n in range(count)], axis=1
    )


def features_kernel(steps, *refs):
    hbm_refs, out_ref, local_refs = refs[:11], refs[11], refs[12:23]
    rows_ref, a_sum, g_sum, blocks, small_sems, sems = refs[23:]
    q, ba_ref, bg_ref, eig_ref, span, owner, length, act, grad, pin, pout = local_refs
    bf16, f32 = jnp.bfloat16, jnp.float32
    count = q.shape[0]
    wa, wg = eig_ref.shape
    rows, part = act.shape[1:]
    n_docs = owner.shape[1]
    n_dev = out_ref.shape[0]
    share = wa // n_dev
    dot = functools.partial(lax.dot_general, preferred_element_type=f32)

    def chunk(k):
        cols = pl.ds(pl.multiple_of(k * part, part), part)
        return [
            pltpu.make_async_copy(
                hbm_refs[7 + i].at[:, cols], local_refs[7 + i].at[k], sems.at[k, i]
            )
            for i in range(4)
        ]

    small = []
    for i in range(7):
        copy = pltpu.make_async_copy(hbm_refs[i], local_refs[i], small_sems.at[i])
        copy.start()
        small.append(copy)
    for k in range(steps):
        for copy in chunk(k):
            copy.start(priority=1)
    a_sum[...] = jnp.zeros_like(a_sum)
    g_sum[...] = jnp.zeros_like(g_sum)

    def write_tiles(first, tiles):
        table = jnp.swapaxes(blocks[: tiles * share], 0, 1)
        for i in range(tiles):
            tile = table[:, i * share : (i + 1) * share]
            out_ref[:, first + i] = tile.astype(bf16)

    def whiten():
        for copy in small[:4]:
            copy.wait()
        for a in range(wa):
            rows_ref[a * count : (a + 1) * count, :] = q[:, a * wg : (a + 1) * wg]
        grid = jnp.concatenate(
            [rows_ref[pl.ds(n, wa, stride=count), :] for n in range(count)], axis=0
        )
        ba, bg = ba_ref[...], bg_ref[...]
        scale = jnp.concatenate([eig_ref[...] + damping] * count, axis=1)
        rotated = split_dot(ba.T, side_by_side(split_dot(grid, bg), count))
        back = split_dot(ba, rotated / scale)
        back = jnp.concatenate(
            [back[:, n * wg : (n + 1) * wg] for n in range(count)], axis=0
        )
        white = split_dot(back, bg.T)
        for r in range(share):
            for n in range(count):
                lo = n * wa + r * n_dev
                blocks[n * share + r] = white[lo : lo + n_dev]
        write_tiles(n_docs, count)

    def add_chunk(k, carry):
        for copy in chunk(k):
            copy.wait()
        a_sum[...] += dot(act[k], pin[k], NT)
        g_sum[...] += dot(grad[k], pout[k], NT)
        return carry

    whiten()
    for copy in small[4:]:
        copy.wait()
    row = lax.broadcasted_iota(jnp.int32, (share, wg), 0)
    lane = lax.broadcasted_iota(jnp.int32, (share, wg), 1)
    each = n_docs // share
    place = row * each + lax.div(lane, wg // each)
    target = jnp.full((share, wg), owner[0, 0], jnp.int32)
    for d in range(1, n_docs):
        target = jnp.where(place == d, owner[0, d], target)
    target = jnp.broadcast_to(target.astype(f32)[None], (n_dev, share, wg))
    out_ref[:, n_docs + count] = target.astype(bf16)
    lax.fori_loop(0, steps - 1, add_chunk, 0)
    add_chunk(steps - 1, 0)
    a_part = a_sum[...].T.astype(bf16).astype(f32)
    g_part = g_sum[...].astype(bf16)
    me = lax.axis_index("seq")
    position = lax.broadcasted_iota(jnp.int32, (wa, rows), 1)
    start = jnp.int32(0)
    spread = []
    for d in range(n_docs):
        end = start + span[0, me, d]
        inside = (position >= start) & (position < end)
        spread.append(jnp.where(inside, a_part, 0.0).astype(bf16))
        start = end
    sums = dot(jnp.concatenate(spread, axis=0), g_part, NN)
    for d in range(n_docs):
        tokens = jnp.full((n_dev, wg), length[0, d], jnp.int32).astype(f32)
        for r in range(share):
            lo = d * wa + r * n_dev
            blocks[d * share + r] = sums[lo : lo + n_dev] / tokens
    write_tiles(0, n_docs)


def partial_kernel(n_docs, block_ref, out_ref, rows_ref, white_ref):
    bf16, f32 = jnp.bfloat16, jnp.float32
    n_dp, n_seq, n_hi = out_ref.shape[:3]
    n_dev, slots, share, wg = block_ref.shape
    count = slots - n_docs - 1
    n_out = n_dev * count // n_seq
    n_lo = n_dp // n_hi
    for d in range(n_docs):
        part = block_ref[:, d].astype(f32).reshape(n_dp, n_seq, share, wg)
        total = part[:, 0]
        for s in range(1, n_seq):
            total += part[:, s]
        rows_ref[d, :n_dp] = total
    for n in range(n_docs, n_docs + count):
        rows_ref[n] = block_ref[:, n].astype(f32)
    part = block_ref[:, n_docs + count].astype(f32)
    rows_ref[n_docs + count, :n_dp] = part.reshape(n_dp, n_seq, share, wg)[:, 0]
    for n in range(count):
        for r in range(share):
            white_ref[r, pl.ds(n, n_dev, stride=count), :] = rows_ref[n_docs + n, :, r]
    docs = jnp.concatenate(
        [
            jnp.concatenate([rows_ref[d, :n_dp, r] for d in range(n_docs)], axis=0)
            for r in range(share)
        ],
        axis=1,
    )
    white = jnp.concatenate([white_ref[r] for r in range(share)], axis=1).astype(bf16)
    each = n_docs // share
    owners = []
    for d in range(n_docs):
        lane = d % each * (wg // each)
        column = rows_ref[n_docs + count, :n_dp, d // each][:, lane : lane + 1]
        owners.append(jnp.broadcast_to(column, (n_dp, n_dev * count)))
    upper = docs.astype(bf16)
    lower = (docs - upper.astype(f32)).astype(bf16)
    both = lax.dot_general(
        jnp.concatenate([upper, lower], axis=0), white, NT, preferred_element_type=f32
    )
    scores = both[: n_docs * n_dp] + both[n_docs * n_dp :]
    routed = []
    for o in range(n_dp):
        row = jnp.zeros((n_dp, n_dev * count), f32)
        for d in range(n_docs):
            mine = owners[d] == float(o)
            row += jnp.where(mine, scores[d * n_dp : (d + 1) * n_dp], 0.0)
        routed.append(row)
    scores = jnp.swapaxes(jnp.stack(routed), 0, 1).reshape(n_dp * n_dp, n_dev * count)
    tall = n_hi * n_dp
    for s in range(n_seq):
        lanes = slice(s * n_out, (s + 1) * n_out)
        packed = jnp.concatenate(
            [scores[lo * tall : (lo + 1) * tall, lanes] for lo in range(n_lo)], axis=1
        )
        for hi in range(n_hi):
            out_ref[:, s, hi, :] = packed[hi * n_dp : (hi + 1) * n_dp].astype(bf16)


def finish_kernel(parts_ref, out_ref):
    n_hi = parts_ref.shape[1]
    n_dp, n_out = out_ref.shape
    total = jnp.sum(parts_ref[...].astype(jnp.float32), axis=0)
    for lo in range(n_dp // n_hi):
        out_ref[lo * n_hi : (lo + 1) * n_hi, :] = total[:, lo * n_out : (lo + 1) * n_out]


def by_features(
    activations,
    out_grads,
    proj_in,
    proj_out,
    queries,
    basis_a,
    basis_g,
    eigen,
    spans,
    doc_owner,
    doc_lengths,
):
    n_dp, n_seq = lax.axis_size("dp"), lax.axis_size("seq")
    n_dev = n_dp * n_seq
    wa, wg = eigen.shape
    count = queries.shape[0]
    share = wa // n_dev
    n_docs = doc_owner.shape[1]
    height = share * (n_docs + count + 1)
    n_out = n_dev * count // n_seq
    n_hi = n_dp * n_out // 128
    bf16, f32 = jnp.bfloat16, jnp.float32
    steps = 5
    part = activations.shape[1] // steps
    vmem = pl.BlockSpec(memory_space=pltpu.VMEM)
    hbm = pl.BlockSpec(memory_space=pltpu.HBM)
    small = (queries, basis_a, basis_g, eigen)
    integers = (spans, doc_owner, doc_lengths)
    large = (activations, out_grads, proj_in, proj_out)
    operands = small + integers + large
    copied = (
        [pltpu.VMEM(x.shape, x.dtype) for x in small]
        + [pltpu.SMEM(x.shape, x.dtype) for x in integers]
        + [pltpu.VMEM((steps, x.shape[0], part), x.dtype) for x in large]
    )
    blocks = pl.pallas_call(
        functools.partial(features_kernel, steps),
        out_shape=jax.ShapeDtypeStruct((n_dev, height // share, share, wg), bf16),
        in_specs=[hbm] * 11,
        out_specs=vmem,
        scratch_shapes=copied
        + [
            pltpu.VMEM((wa * count, wg), f32),
            pltpu.VMEM((activations.shape[0], wa), f32),
            pltpu.VMEM((activations.shape[0], wg), f32),
            pltpu.VMEM((share * max(n_docs, count), n_dev, wg), f32),
            pltpu.SemaphoreType.DMA((7,)),
            pltpu.SemaphoreType.DMA((steps, 4)),
        ],
        compiler_params=pltpu.CompilerParams(vmem_limit_bytes=features_bytes),
        name="features",
    )(*(pltpu.with_memory_space_constraint(x, pltpu.HBM) for x in operands))
    everywhere = functools.partial(
        lax.all_to_all,
        axis_name=("dp", "seq"),
        split_axis=0,
        concat_axis=0,
        tiled=True,
    )
    blocks = everywhere(blocks)
    parts = pl.pallas_call(
        functools.partial(partial_kernel, n_docs),
        out_shape=jax.ShapeDtypeStruct((n_dp, n_seq, n_hi, 128), bf16),
        in_specs=[vmem],
        out_specs=vmem,
        scratch_shapes=[
            pltpu.VMEM((height // share, n_dev, share, wg), f32),
            pltpu.VMEM((share, n_dev * count, wg), f32),
        ],
        compiler_params=pltpu.CompilerParams(vmem_limit_bytes=small_bytes),
        name="partial",
    )(blocks)
    parts = everywhere(parts.reshape(n_dev, n_hi, 128))
    result = pl.pallas_call(
        finish_kernel,
        out_shape=jax.ShapeDtypeStruct((n_dp, n_out), f32),
        in_specs=[vmem],
        out_specs=vmem,
        compiler_params=pltpu.CompilerParams(vmem_limit_bytes=small_bytes),
        name="finish",
    )(parts)
    return result[None]


def by_rows(
    activations,
    out_grads,
    proj_in,
    proj_out,
    queries,
    basis_a,
    basis_g,
    eigen,
    spans,
    doc_owner,
    doc_lengths,
):
    n_dp, n_seq = lax.axis_size("dp"), lax.axis_size("seq")
    n_dev = n_dp * n_seq
    rows, width = activations.shape
    wa, wg = eigen.shape
    count = queries.shape[0]
    share = wa // n_seq
    steps = 5
    part = width // steps
    bf16, f32 = jnp.bfloat16, jnp.float32
    params = pltpu.CompilerParams(vmem_limit_bytes=vmem_bytes)
    vmem = pl.BlockSpec(memory_space=pltpu.VMEM)
    hbm = pl.BlockSpec(memory_space=pltpu.HBM)

    outgoing = pl.pallas_call(
        whiten_kernel,
        out_shape=jax.ShapeDtypeStruct((n_dp, n_seq, count, share, wg), bf16),
        in_specs=[vmem] * 4,
        out_specs=vmem,
        scratch_shapes=[pltpu.VMEM((wa * count, wg), f32)],
        compiler_params=params,
        name="whiten",
    )(queries, basis_a, basis_g, eigen)
    white = lax.all_to_all(
        outgoing.reshape(n_dev, count, share, wg),
        ("dp", "seq"),
        split_axis=0,
        concat_axis=0,
        tiled=True,
    )

    docs = pl.pallas_call(
        functools.partial(docs_kernel, steps),
        out_shape=jax.ShapeDtypeStruct((n_dp, n_seq, share, wg), bf16),
        in_specs=[hbm] * 8,
        out_specs=vmem,
        scratch_shapes=[
            pltpu.VMEM((steps, rows, part), bf16),
            pltpu.VMEM((steps, rows, part), bf16),
            pltpu.VMEM((steps, wa, part), bf16),
            pltpu.VMEM((steps, wg, part), bf16),
            pltpu.SMEM(spans.shape, jnp.int32),
            pltpu.SMEM(doc_owner.shape, jnp.int32),
            pltpu.SMEM(doc_lengths.shape, jnp.int32),
            pltpu.SemaphoreType.DMA((steps, 4)),
            pltpu.SemaphoreType.DMA((3,)),
        ],
        compiler_params=params,
        name="docs",
    )(
        spans,
        doc_owner,
        doc_lengths,
        activations,
        out_grads,
        proj_in,
        proj_out,
        outgoing,
    )
    docs = lax.all_to_all(
        docs.reshape(n_dev, share, wg),
        ("dp", "seq"),
        split_axis=0,
        concat_axis=0,
        tiled=True,
    )

    n_query = n_dev * count
    n_out = n_query // n_seq
    parts = pl.pallas_call(
        score_kernel,
        out_shape=[jax.ShapeDtypeStruct((n_dp, n_out), f32)] * n_seq,
        in_specs=[vmem] * 2,
        out_specs=[vmem] * n_seq,
        scratch_shapes=[pltpu.VMEM((n_query, n_dp * share), f32)],
        compiler_params=params,
        name="score",
    )(docs.reshape(n_dp, n_seq, share, wg), white.reshape(n_query, share, wg))
    result = parts[0]
    for k in range(n_seq - 1, 0, -1):
        pairs = [(i, i ^ k) for i in range(n_seq)]
        result = result + lax.ppermute(parts[k], "seq", pairs)
    return result[None]


def per_device(*args):
    n_dp, n_seq = lax.axis_size("dp"), lax.axis_size("seq")
    n_dev = n_dp * n_seq
    wa, wg = args[7].shape
    count = args[4].shape[0]
    share = wa // n_dev
    n_out = n_dp * count
    fits = (
        share > 0
        and share * n_dev == wa
        and wg == 128
        and n_dp % 8 == 0
        and n_dp <= 256
        and args[9].shape[1] % share == 0
        and 128 % n_out == 0
        and n_dp * n_out % 128 == 0
    )
    return (by_features if fits else by_rows)(*args)


def solution(mesh):
    return jax.shard_map(
        per_device,
        mesh=mesh,
        in_specs=(
            P(("dp", "seq"), None),
            P(("dp", "seq"), None),
            P(),
            P(),
            P(("dp", "seq"), None),
            P(),
            P(),
            P(),
            P("dp", None, None),
            P("dp", None),
            P("dp", None),
        ),
        out_specs=P("dp", None, "seq"),
        check_vma=False,
    )
```
